32 devices in a mesh: seq: 8 (over z, y), head: 4 (over x, core).
Axes of the slice: x: 2, y: 2, z: 4, core: 2. Of those that a mesh axis runs over, the one named last changes fastest.
Arguments:
- queries: bfloat16 [2048, 16, 128], P('seq', 'head'), may hold values from -42 to 42, as said below
- keys: bfloat16 [2048, 4, 128], P('seq', 'head'), may hold values from -6 to 6
- values: bfloat16 [2048, 4, 128], P('seq', 'head'), may hold values from -6 to 6
- feat_q: bfloat16 [16, 128, 128], P('head'), may hold values from -0.5 to 0.5
- feat_k: bfloat16 [16, 128, 128], P('head'), may hold values from -0.5 to 0.5
- samples: int32 [8], replicated, may hold values from 0 to 1
Outputs:
- student: bfloat16 [2048, 16, 128], P('seq', 'head')
- teacher: float32 [8, 128, 16, 128], P('seq', None, 'head')
- loss: float32 [], replicated
The draws below stay inside these ranges and needn't reach their ends.
Inputs may be any that keep to these rules, and one draw needn't show every extreme that they name: `queries`: query vectors; some may be large multiples of earlier key vectors.
All inputs are finite; a program needn't handle non-finite values.
Results may differ from the reference program's by a relative error of at most 0.009.
Values may be sent and summed in bfloat16 or wider, within the bound.
A program may use at most 64 MiB of HBM per device.

```python
import jax
import jax.numpy as jnp
from jax import lax

HD = 128
FEAT = 128
QH_DEV = 4
BLOCK = 128
TOK_DEV = 256
LENGTH = 2048
Q_HEADS = 16
KV_HEADS = 4
N_SEQ = 8


def draw_pair(key):
    key_query = jax.random.fold_in(key, 11)
    key_key = jax.random.fold_in(key, 23)
    query_rows = jnp.clip(jax.random.normal(key_query, (LENGTH, Q_HEADS, HD), jnp.float32), -6.0, 6.0)
    key_rows = jnp.clip(jax.random.normal(key_key, (LENGTH, KV_HEADS, HD), jnp.float32), -6.0, 6.0)
    return (query_rows, key_rows)


def draw_queries(key, part):
    query_rows, key_rows = draw_pair(key)
    return query_rows.astype(jnp.bfloat16)


def draw_keys(key, part):
    query_rows, key_rows = draw_pair(key)
    return key_rows.astype(jnp.bfloat16)


def set_ends(drawn, stream_key, least, high):
    dims = drawn.shape
    index_at = [jax.random.randint(jax.random.fold_in(stream_key, axis), (), 0, dims[axis]) for axis in range(len(dims))]
    drawn = drawn.at[tuple(index_at)].set(least)
    longest = dims.index(max(dims))
    index_at[longest] = (index_at[longest] + 1) % dims[longest]
    return drawn.at[tuple(index_at)].set(high)


def shard_levels(own_key, shape, split, low, largest):
    level = 1.0
    for position, parts in split:
        steps = jax.random.uniform(jax.random.fold_in(jax.random.fold_in(own_key, 6), position), (parts,), jnp.float32, low / len(split), largest / len(split))
        level = level * jnp.repeat(jnp.exp(steps), shape[position] // parts).reshape((-1,) + (1,) * (len(shape) - 1 - position))
    return level


def gaussian(own_key, shape, spread, reach, shards=(), kind=jnp.bfloat16):
    drawn = spread * jax.random.normal(own_key, shape, jnp.float32)
    if shards:
        drawn = drawn * shard_levels(own_key, shape, shards, -0.22, 0.18)
    return jnp.clip(drawn, -reach, reach).astype(kind)


def setup_inputs(seed: int = 0) -> dict:
    key_list = jax.random.split(jax.random.key(seed), 7)
    return {
        "queries": draw_queries(jax.random.fold_in(key_list[6], 71), 0),
        "keys": draw_keys(jax.random.fold_in(key_list[6], 71), 0),
        "values": gaussian(key_list[2], (LENGTH, KV_HEADS, HD), 1.0, 6.0, ((0, 8), (1, 4))),
        "feat_q": gaussian(key_list[3], (Q_HEADS, HD, FEAT), HD ** -0.5, 0.5, ((0, 4),)),
        "feat_k": gaussian(key_list[4], (Q_HEADS, HD, FEAT), HD ** -0.5, 0.5, ((0, 4),)),
        "samples": set_ends(jax.random.randint(key_list[5], (N_SEQ,), 0, TOK_DEV // BLOCK), jax.random.fold_in(key_list[5], 1), 0, (TOK_DEV // BLOCK) - 1).astype(jnp.int32),
    }


PRECISE = lax.Precision.HIGHEST

def features(logits):
    return jnp.concatenate([jax.nn.softmax(logits, axis=-1), jax.nn.softmax(-logits, axis=-1)], axis=-1).astype(jnp.bfloat16)

def reference(queries, keys, values, feat_q, feat_k, samples):
    length, head_count, head_width = queries.shape
    kv_group = jnp.arange(head_count) // QH_DEV
    block_count = length // BLOCK
    query_blocks = queries.reshape(block_count, BLOCK, head_count, head_width)
    key_blocks = keys.reshape(block_count, BLOCK, keys.shape[1], head_width)
    value_blocks = values.reshape(block_count, BLOCK, values.shape[1], head_width)
    feat_q32 = feat_q.astype(jnp.float32)
    feat_k32 = feat_k.astype(jnp.float32)
    causal = jnp.arange(BLOCK)[:, None] >= jnp.arange(BLOCK)[None, :]

    def advance(running, inputs):
        kv_state, key_total = running
        query_part, key_part, value_part = inputs
        key_wide = key_part[:, kv_group].astype(jnp.float32)
        value_wide = value_part[:, kv_group].astype(jnp.float32)
        phi_q = features(jnp.einsum('lhd,hdf->lhf', query_part.astype(jnp.float32), feat_q32, precision=PRECISE)).astype(jnp.float32)
        phi_k = features(jnp.einsum('lhd,hdf->lhf', key_wide, feat_k32, precision=PRECISE)).astype(jnp.float32)
        kernel = jnp.einsum('ihf,jhf->hij', phi_q, phi_k, precision=PRECISE)
        kernel = jnp.where(causal[None], kernel, 0.0)
        kernel_low = lax.optimization_barrier(kernel.astype(jnp.bfloat16)).astype(jnp.float32)
        numer = jnp.einsum('hij,jhd->ihd', kernel_low, value_wide, precision=PRECISE)
        numer = numer + jnp.einsum('ihf,hfd->ihd', phi_q, kv_state, precision=PRECISE)
        denom = lax.optimization_barrier(jnp.sum(kernel, axis=2)).T + jnp.einsum('ihf,hf->ih', phi_q, key_total, precision=PRECISE)
        result = (numer / denom[..., None]).astype(jnp.bfloat16)
        kv_state = kv_state + jnp.einsum('jhf,jhd->hfd', phi_k, value_wide, precision=PRECISE)
        key_total = key_total + lax.optimization_barrier(jnp.sum(phi_k, axis=0))
        return ((kv_state, key_total), result)
    start_state = jnp.zeros((head_count, 2 * FEAT, head_width), jnp.float32)
    start_total = jnp.zeros((head_count, 2 * FEAT), jnp.float32)
    ignored, student_blocks = lax.scan(advance, (start_state, start_total), (query_blocks, key_blocks, value_blocks))
    student = student_blocks.reshape(length, head_count, head_width)
    keys32 = keys.astype(jnp.float32)
    values32 = values.astype(jnp.float32)
    inv_root = 1.0 / jnp.sqrt(jnp.float32(head_width))
    key_places = jnp.arange(length)

    def teach(stretch):
        row_first = (stretch * TOK_DEV + samples[stretch] * BLOCK).astype(jnp.int32)
        query_rows = lax.dynamic_slice_in_dim(queries, row_first, BLOCK, 0).astype(jnp.float32)
        query_rows = query_rows.reshape(BLOCK, keys.shape[1], QH_DEV, head_width)
        row_places = row_first + jnp.arange(BLOCK)
        scores = jnp.einsum('bgnd,kgd->gnbk', query_rows, keys32, precision=PRECISE) * inv_root
        live = key_places[None, :] <= row_places[:, None]
        scores = jnp.where(live[None, None], scores, -jnp.inf)
        peak = lax.optimization_barrier(jnp.max(scores, axis=-1, keepdims=True))
        weights = jnp.exp(scores - peak)
        totals = lax.optimization_barrier(jnp.sum(weights, axis=-1))
        rounded = lax.optimization_barrier(weights.astype(jnp.bfloat16)).astype(jnp.float32)
        mixed = jnp.einsum('gnbk,kgd->gnbd', rounded, values32, precision=PRECISE) / totals[..., None]
        mixed = jnp.transpose(mixed, (2, 0, 1, 3)).reshape(BLOCK, head_count, head_width)
        student_rows = lax.dynamic_slice_in_dim(student, row_first, BLOCK, 0).astype(jnp.float32)
        gap = student_rows - mixed
        return (mixed, jnp.sum(gap * gap))
    teacher, squares = lax.map(teach, jnp.arange(samples.shape[0]).astype(jnp.int32))
    loss = jnp.sum(squares) / (samples.shape[0] * BLOCK * head_count * head_width)
    return (student, teacher, loss)
```

```python
import functools

import jax
import jax.numpy as jnp
from jax import lax
from jax.experimental import pallas as pl
from jax.experimental.pallas import tpu as pltpu
from jax.sharding import PartitionSpec as P

BLOCK = 128
MASKED = -1e30
LOG2E = 1.4426950408889634
NT = (((1,), (1,)), ((), ()))


def dot(a, b):
    return jnp.dot(a, b, preferred_element_type=jnp.float32)


def soft_pair(logits, axis):
    up = jnp.exp(logits - jnp.max(logits, axis=axis, keepdims=True))
    down = jnp.exp(jnp.min(logits, axis=axis, keepdims=True) - logits)
    up = up * (1.0 / jnp.sum(up, axis=axis, keepdims=True))
    down = down * (1.0 / jnp.sum(down, axis=axis, keepdims=True))
    return jnp.concatenate([up, down], axis=axis).astype(jnp.bfloat16)


def kernel(
    n, nh, q_hbm, k_hbm, v_hbm, fq_hbm, fk_hbm, samples, student, teacher, loss,
    kv, q_raw, fq, fk, fk_t, rows32, qs_t, phi_q, state, num, den, top, tot, acc, out32, heads_part, seq_part,
    local_sem, recv_sem, send_sem, head_send, head_recv, seq_send, seq_recv,
):
    tok, width = k_hbm.shape
    heads = fq.shape[0]
    s, hd = lax.axis_index("seq"), lax.axis_index("head")
    outer, y = s // 2, s % 2
    last = n // 2 - 1
    partner = s + 1 - 2 * y
    own = (k_hbm, v_hbm)

    local = [
        pltpu.make_async_copy(src, dst, local_sem.at[i])
        for i, (src, dst) in enumerate(
            [(q_hbm, q_raw), (fq_hbm, fq), (fk_hbm, fk), (k_hbm, kv.at[s, 0]), (v_hbm, kv.at[s, 1])]
        )
    ]
    for copy in local:
        copy.start()

    barrier = pltpu.get_barrier_semaphore()
    for i in range(1, n):
        pl.semaphore_signal(barrier, inc=1, device_id={"seq": lax.rem(s + i, n)}, device_id_type=pl.DeviceIdType.MESH)
    for i in range(1, nh):
        pl.semaphore_signal(barrier, inc=1, device_id={"head": lax.rem(hd + i, nh)}, device_id_type=pl.DeviceIdType.MESH)
    pl.semaphore_wait(barrier, n - 1 + nh - 1)

    def hop(src, slot, j, way, target):
        return pltpu.make_async_remote_copy(
            src_ref=src, dst_ref=kv.at[slot, j], send_sem=send_sem.at[way, slot, j],
            recv_sem=recv_sem.at[slot, j], device_id={"seq": target}, device_id_type=pl.DeviceIdType.MESH,
        )

    @pl.when(outer < last)
    def _():
        for j in range(2):
            hop(own[j], s, j, 0, s + 2).start()

    @pl.when(y == 0)
    def _():
        for j in range(2):
            hop(own[j], s, j, 1, partner).start()

    pick = samples[s]

    def chosen(rows):
        block = rows[:BLOCK]
        for b in range(1, tok // BLOCK):
            block = jnp.where(pick == b, rows[b * BLOCK:(b + 1) * BLOCK], block)
        return block

    def key_features(keys, h):
        logits = lax.dot_general(fk_t[h * 128:(h + 1) * 128, :], keys, NT, preferred_element_type=jnp.float32)
        return soft_pair(logits, 0)

    def teach(keys, values, live):
        values_t = values.astype(jnp.float32).T.astype(jnp.bfloat16)
        for c in range(heads // 2):
            cols = slice(c * 2 * BLOCK, (c + 1) * 2 * BLOCK)
            scores = dot(keys, qs_t[:, cols]) * (LOG2E / width ** 0.5)
            if live is not None:
                scores = jnp.where(live, scores, MASKED)
            peak = jnp.max(scores, axis=0, keepdims=True)
            if live is None:
                old = top[:, cols]
                peak = jnp.maximum(old, peak)
                fade = jnp.exp2(old - peak)
            weights = jnp.exp2(scores - peak)
            total = jnp.sum(weights, axis=0, keepdims=True)
            mixed = dot(values_t, weights.astype(jnp.bfloat16))
            if live is None:
                total = total + tot[:, cols] * fade
                mixed = mixed + acc[:, cols] * fade
            top[:, cols] = peak
            tot[:, cols] = total
            acc[:, cols] = mixed

    def wide(values):
        return jnp.concatenate([values, jnp.ones_like(values)], axis=1)

    def absorb(slot):
        keys, values = kv[slot, 0], kv[slot, 1]
        teach(keys, values, None)
        values_wide = wide(values)
        for h in range(heads):
            state[h] += dot(key_features(keys, h), values_wide)

    state[...] = jnp.zeros_like(state)
    for copy in local:
        copy.wait()
    rows32[...] = q_raw[...].astype(jnp.float32)
    for h in range(heads):
        mine = rows32[pl.ds(h, tok, stride=heads), :]
        qs_t[:, h * BLOCK:(h + 1) * BLOCK] = chosen(mine).T.astype(jnp.bfloat16)
        fk_t[h * 128:(h + 1) * 128, :] = fk[h].astype(jnp.float32).T.astype(jnp.bfloat16)
        phi_q[h] = soft_pair(dot(mine.astype(jnp.bfloat16), fq[h]), 1)
    keys, values = kv[s, 0], kv[s, 1]
    place = lax.broadcasted_iota(jnp.int32, (tok, 2 * BLOCK), 0)
    row = lax.broadcasted_iota(jnp.int32, (tok, 2 * BLOCK), 1) % BLOCK + pick * BLOCK
    teach(keys, values, place <= row)
    causal = lax.broadcasted_iota(jnp.int32, (tok, tok), 0) >= lax.broadcasted_iota(jnp.int32, (tok, tok), 1)
    for h in range(heads):
        inner = jnp.where(causal, dot(phi_q[h], key_features(keys, h)), 0.0)
        num[h] = dot(inner.astype(jnp.bfloat16), values)
        den[h] = jnp.broadcast_to(jnp.sum(inner, axis=1, keepdims=True), (tok, width))

    @pl.when(y == 1)
    def _():
        for j in range(2):
            hop(own[j], partner, j, 1, partner).wait_recv()
        absorb(partner)

    def lap(d, carry):
        near, far = s - 2 * d, partner - 2 * d
        for j in range(2):
            hop(kv.at[near, j], near, j, 0, s).wait_recv()

            @pl.when(outer < last)
            def _():
                hop(kv.at[near, j], near, j, 0, s + 2).start()

            hop(kv.at[near, j], near, j, 1, partner).start()
        absorb(near)
        for j in range(2):
            hop(kv.at[far, j], far, j, 1, partner).wait_recv()
        absorb(far)
        return carry

    lax.fori_loop(1, outer + 1, lap, 0)

    part = jnp.zeros((8, width), jnp.float32)
    for h in range(heads):
        cols = slice(h * BLOCK, (h + 1) * BLOCK)
        inter = dot(phi_q[h], state[h].astype(jnp.bfloat16))
        result = (num[h] + inter[:, :width]) / (den[h] + inter[:, width:])
        result = result.astype(jnp.bfloat16).astype(jnp.float32)
        out32[pl.ds(h, tok, stride=heads), :] = result
        mixed = (acc[:, cols] / tot[:, cols]).T
        teacher[pl.ds(h, BLOCK, stride=heads), :] = mixed
        gap = chosen(result) - mixed
        part = part + jnp.sum((gap * gap).reshape(BLOCK // 8, 8, width), axis=0)

    def spread(buf, mine, count, axis, send, recv, i):
        return pltpu.make_async_remote_copy(
            src_ref=buf.at[mine], dst_ref=buf.at[mine], send_sem=send.at[i], recv_sem=recv.at[i],
            device_id={axis: lax.rem(mine + i, count)}, device_id_type=pl.DeviceIdType.MESH,
        )

    heads_part[hd] = part
    copies = [spread(heads_part, hd, nh, "head", head_send, head_recv, i) for i in range(1, nh)]
    for copy in copies:
        copy.start()
    student[...] = out32[...].astype(jnp.bfloat16)
    for copy in copies:
        copy.wait()
    seq_part[s] = jnp.sum(heads_part[...], axis=0)
    copies = [spread(seq_part, s, n, "seq", seq_send, seq_recv, i) for i in range(1, n)]
    for copy in copies:
        copy.start()

    @pl.when(outer < last)
    def _():
        for j in range(2):
            hop(own[j], s, j, 0, s + 2).wait_send()

    @pl.when(y == 0)
    def _():
        for j in range(2):
            hop(own[j], s, j, 1, partner).wait_send()

    def drain(d, carry):
        near = s - 2 * d
        for j in range(2):
            @pl.when(outer < last)
            def _():
                hop(kv.at[near, j], near, j, 0, s + 2).wait_send()

            hop(kv.at[near, j], near, j, 1, partner).wait_send()
        return carry

    lax.fori_loop(1, outer + 1, drain, 0)
    for copy in copies:
        copy.wait()
    loss[0, 0] = jnp.sum(seq_part[...]) * (1.0 / (n * nh * BLOCK * heads * width))


def on_device(n, nh, queries, keys, values, feat_q, feat_k, samples):
    tok, heads, width = queries.shape
    bf16, f32 = jnp.bfloat16, jnp.float32
    anywhere = pl.BlockSpec(memory_space=pl.ANY)
    in_vmem = pl.BlockSpec(memory_space=pltpu.VMEM)
    in_smem = pl.BlockSpec(memory_space=pltpu.SMEM)
    dma = pltpu.SemaphoreType.DMA
    student, teacher, loss = pl.pallas_call(
        functools.partial(kernel, n, nh),
        out_shape=(
            jax.ShapeDtypeStruct((tok * heads, width), bf16),
            jax.ShapeDtypeStruct((BLOCK * heads, width), f32),
            jax.ShapeDtypeStruct((1, 1), f32),
        ),
        in_specs=[anywhere] * 5 + [in_smem],
        out_specs=(in_vmem, in_vmem, in_smem),
        scratch_shapes=[
            pltpu.VMEM((n, 2, tok, width), bf16),
            pltpu.VMEM((tok * heads, width), bf16),
            pltpu.VMEM(feat_q.shape, bf16),
            pltpu.VMEM(feat_k.shape, bf16),
            pltpu.VMEM((heads * 128, width), bf16),
            pltpu.VMEM((tok * heads, width), f32),
            pltpu.VMEM((width, heads * BLOCK), bf16),
            pltpu.VMEM((heads, tok, 256), bf16),
            pltpu.VMEM((heads, 256, 2 * width), f32),
            pltpu.VMEM((heads, tok, width), f32),
            pltpu.VMEM((heads, tok, width), f32),
            pltpu.VMEM((1, heads * BLOCK), f32),
            pltpu.VMEM((1, heads * BLOCK), f32),
            pltpu.VMEM((width, heads * BLOCK), f32),
            pltpu.VMEM((tok * heads, width), f32),
            pltpu.VMEM((nh, 8, width), f32),
            pltpu.VMEM((n, 8, width), f32),
            dma((5,)), dma((n, 2)), dma((2, n, 2)), dma((nh,)), dma((nh,)), dma((n,)), dma((n,)),
        ],
        compiler_params=pltpu.CompilerParams(
            collective_id=0, has_side_effects=True, vmem_limit_bytes=60 * 1024 * 1024
        ),
    )(
        queries.reshape(tok * heads, width), keys.reshape(tok, width), values.reshape(tok, width),
        feat_q, feat_k, samples,
    )
    return student.reshape(tok, heads, width), teacher.reshape(1, BLOCK, heads, width), loss.reshape(())


def solution(mesh):
    in_specs = (
        P("seq", "head", None),
        P("seq", "head", None),
        P("seq", "head", None),
        P("head", None, None),
        P("head", None, None),
        P(),
    )
    out_specs = (P("seq", "head", None), P("seq", None, "head", None), P())
    return jax.shard_map(
        functools.partial(on_device, mesh.shape["seq"], mesh.shape["head"]),
        mesh=mesh, in_specs=in_specs, out_specs=out_specs, check_vma=False,
    )
```

```python
import functools

import jax
import jax.numpy as jnp
from jax import lax
from jax.experimental import pallas as pl
from jax.experimental.pallas import tpu as pltpu
from jax.sharding import PartitionSpec as P

BLOCK = 128
MASKED = -1e30
LOG2E = 1.4426950408889634
NT = (((1,), (1,)), ((), ()))


def dot(a, b):
    return jnp.dot(a, b, preferred_element_type=jnp.float32)


def soft_pair(logits, axis):
    up = jnp.exp(logits - jnp.max(logits, axis=axis, keepdims=True))
    down = jnp.exp(jnp.min(logits, axis=axis, keepdims=True) - logits)
    up = up * (1.0 / jnp.sum(up, axis=axis, keepdims=True))
    down = down * (1.0 / jnp.sum(down, axis=axis, keepdims=True))
    return jnp.concatenate([up, down], axis=axis).astype(jnp.bfloat16)


def kernel(
    n, nh, q_hbm, k_hbm, v_hbm, fq_hbm, fk_hbm, samples, out32, teacher, loss,
    kv, q_raw, fq, fk, fk_t, rows32, qs_t, phi_q, state, num, den, top, tot, acc, column, below, plane, total,
    local_sem, recv_sem, send_sem, up_sem, plane_send, plane_recv, down_send, down_recv,
):
    tok, width = k_hbm.shape
    heads = fq.shape[0]
    s, hd = lax.axis_index("seq"), lax.axis_index("head")
    outer, y = s // 2, s % 2
    last = n // 2 - 1
    partner = s + 1 - 2 * y
    own = (k_hbm, v_hbm)

    local = [
        pltpu.make_async_copy(src, dst, local_sem.at[i])
        for i, (src, dst) in enumerate(
            [(q_hbm, q_raw), (fq_hbm, fq), (fk_hbm, fk), (k_hbm, kv.at[s, 0]), (v_hbm, kv.at[s, 1])]
        )
    ]
    for copy in local:
        copy.start()

    barrier = pltpu.get_barrier_semaphore()
    mate = y * nh + hd

    def plane_device(i):
        other = lax.rem(mate + i, 2 * nh)
        return {"seq": 2 * outer + other // nh, "head": lax.rem(other, nh)}

    for i in range(1, 2 * nh):
        pl.semaphore_signal(barrier, inc=1, device_id=plane_device(i), device_id_type=pl.DeviceIdType.MESH)

    @pl.when(outer > 0)
    def _():
        pl.semaphore_signal(barrier, inc=1, device_id={"seq": s - 2}, device_id_type=pl.DeviceIdType.MESH)

    @pl.when(outer < last)
    def _():
        pl.semaphore_signal(barrier, inc=1, device_id={"seq": s + 2}, device_id_type=pl.DeviceIdType.MESH)

    pl.semaphore_wait(barrier, 2 * nh - 1 + jnp.minimum(outer, 1) + jnp.minimum(last - outer, 1))

    def hop(src, slot, j, way, target):
        return pltpu.make_async_remote_copy(
            src_ref=src, dst_ref=kv.at[slot, j], send_sem=send_sem.at[way, slot, j],
            recv_sem=recv_sem.at[slot, j], device_id={"seq": target}, device_id_type=pl.DeviceIdType.MESH,
        )

    @pl.when(outer < last)
    def _():
        for j in range(2):
            hop(own[j], s, j, 0, s + 2).start()

    @pl.when(y == 0)
    def _():
        for j in range(2):
            hop(own[j], s, j, 1, partner).start()

    pick = samples[s]

    def chosen(rows):
        block = rows[:BLOCK]
        for b in range(1, tok // BLOCK):
            block = jnp.where(pick == b, rows[b * BLOCK:(b + 1) * BLOCK], block)
        return block

    def key_features(keys, h):
        logits = lax.dot_general(fk_t[h * 128:(h + 1) * 128, :], keys, NT, preferred_element_type=jnp.float32)
        return soft_pair(logits, 0)

    def weigh(keys, live):
        out = []
        for c in range(heads // 2):
            cols = slice(c * 2 * BLOCK, (c + 1) * 2 * BLOCK)
            scores = dot(keys, qs_t[:, cols]) * (LOG2E / width ** 0.5)
            if live is not None:
                scores = jnp.where(live, scores, MASKED)
            peak = jnp.max(scores, axis=0, keepdims=True)
            fade = None
            if live is None:
                old = top[:, cols]
                peak = jnp.maximum(old, peak)
                fade = jnp.exp2(old - peak)
            weights = jnp.exp2(scores - peak)
            part = jnp.sum(weights, axis=0, keepdims=True)
            top[:, cols] = peak
            tot[:, cols] = part if live is not None else part + tot[:, cols] * fade
            out.append((cols, weights.astype(jnp.bfloat16), fade))
        return out

    def mix(weighed, values):
        values_t = values.astype(jnp.float32).T.astype(jnp.bfloat16)
        for cols, weights, fade in weighed:
            mixed = dot(values_t, weights)
            acc[:, cols] = mixed if fade is None else mixed + acc[:, cols] * fade

    def arrived(slot, j):
        hop(kv.at[slot, j], slot, j, 0, partner).wait_recv()

    def absorb(slot, wait):
        if wait:
            arrived(slot, 0)
        keys = kv[slot, 0]
        weighed = weigh(keys, None)
        features = [key_features(keys, h) for h in range(heads)]
        if wait:
            arrived(slot, 1)
        values = kv[slot, 1]
        mix(weighed, values)
        values_wide = jnp.concatenate([values, jnp.ones_like(values)], axis=1)
        for h in range(heads):
            state[h] += dot(features[h], values_wide)

    def relay(slot):
        for j in range(2):
            arrived(slot, j)

            @pl.when(outer < last)
            def _():
                hop(kv.at[slot, j], slot, j, 0, s + 2).start()

            hop(kv.at[slot, j], slot, j, 1, partner).start()

    state[...] = jnp.zeros_like(state)
    for copy in local:
        copy.wait()
    rows32[...] = q_raw[...].astype(jnp.float32)
    for h in range(heads):
        mine = rows32[pl.ds(h, tok, stride=heads), :]
        qs_t[:, h * BLOCK:(h + 1) * BLOCK] = chosen(mine).T.astype(jnp.bfloat16)
        fk_t[h * 128:(h + 1) * 128, :] = fk[h].astype(jnp.float32).T.astype(jnp.bfloat16)
        phi_q[h] = soft_pair(dot(mine.astype(jnp.bfloat16), fq[h]), 1)

    @pl.when(outer > 0)
    def _():
        relay(s - 2)

    keys, values = kv[s, 0], kv[s, 1]
    place = lax.broadcasted_iota(jnp.int32, (tok, 2 * BLOCK), 0)
    row = lax.broadcasted_iota(jnp.int32, (tok, 2 * BLOCK), 1) % BLOCK + pick * BLOCK
    mix(weigh(keys, place <= row), values)
    causal = lax.broadcasted_iota(jnp.int32, (tok, tok), 0) >= lax.broadcasted_iota(jnp.int32, (tok, tok), 1)
    for h in range(heads):
        inner = jnp.where(causal, dot(phi_q[h], key_features(keys, h)), 0.0)
        num[h] = dot(inner.astype(jnp.bfloat16), values)
        den[h] = jnp.broadcast_to(jnp.sum(inner, axis=1, keepdims=True), (tok, width))

    @pl.when(y == 1)
    def _():
        absorb(partner, True)

    def lap(d, carry):
        absorb(s - 2 * d, False)

        @pl.when(d < outer)
        def _():
            relay(s - 2 * d - 2)

        absorb(partner - 2 * d, True)
        return carry

    lax.fori_loop(1, outer + 1, lap, 0)

    part = jnp.zeros((8, width), jnp.float32)
    for h in range(heads):
        cols = slice(h * BLOCK, (h + 1) * BLOCK)
        inter = dot(phi_q[h], state[h].astype(jnp.bfloat16))
        result = (num[h] + inter[:, :width]) / (den[h] + inter[:, width:])
        result = result.astype(jnp.bfloat16).astype(jnp.float32)
        out32[pl.ds(h, tok, stride=heads), :] = result
        mixed = (acc[:, cols] / tot[:, cols]).T
        teacher[pl.ds(h, BLOCK, stride=heads), :] = mixed
        gap = chosen(result) - mixed
        part = part + jnp.sum((gap * gap).reshape(BLOCK // 8, 8, width), axis=0)

    def send(src, dst, send_sem, recv_sem, device):
        return pltpu.make_async_remote_copy(
            src_ref=src, dst_ref=dst, send_sem=send_sem, recv_sem=recv_sem,
            device_id=device, device_id_type=pl.DeviceIdType.MESH,
        )

    upward = send(column, below, up_sem.at[0], up_sem.at[1], {"seq": s + 2})
    across = [
        send(plane.at[mate], plane.at[mate], plane_send.at[i], plane_recv.at[i], plane_device(i))
        for i in range(1, 2 * nh)
    ]
    downward = [
        send(total, total, down_send.at[i], down_recv.at[0], {"seq": s - 2 * i}) for i in range(1, last + 1)
    ]
    column[...] = part

    @pl.when(outer > 0)
    def _():
        upward.wait_recv()
        column[...] += below[...]

    @pl.when(outer < last)
    def _():
        upward.start()

    @pl.when(outer == last)
    def _():
        plane[mate] = column[...]
        for copy in across:
            copy.start()
        for copy in across:
            copy.wait()
        total[...] = jnp.sum(plane[...], axis=0)
        for copy in downward:
            copy.start()

    @pl.when(outer < last)
    def _():
        for j in range(2):
            hop(own[j], s, j, 0, s + 2).wait_send()

    @pl.when(y == 0)
    def _():
        for j in range(2):
            hop(own[j], s, j, 1, partner).wait_send()

    def drain(d, carry):
        near = s - 2 * d
        for j in range(2):
            @pl.when(outer < last)
            def _():
                hop(kv.at[near, j], near, j, 0, s + 2).wait_send()

            hop(kv.at[near, j], near, j, 1, partner).wait_send()
        return carry

    lax.fori_loop(1, outer + 1, drain, 0)

    @pl.when(outer == last)
    def _():
        for copy in downward:
            copy.wait_send()

    @pl.when(outer < last)
    def _():
        upward.wait_send()
        downward[0].wait_recv()

    loss[0, 0] = jnp.sum(total[...]) * (1.0 / (n * nh * BLOCK * heads * width))


def on_device(n, nh, queries, keys, values, feat_q, feat_k, samples):
    tok, heads, width = queries.shape
    bf16, f32 = jnp.bfloat16, jnp.float32
    anywhere = pl.BlockSpec(memory_space=pl.ANY)
    in_vmem = pl.BlockSpec(memory_space=pltpu.VMEM)
    in_smem = pl.BlockSpec(memory_space=pltpu.SMEM)
    dma = pltpu.SemaphoreType.DMA
    student, teacher, loss = pl.pallas_call(
        functools.partial(kernel, n, nh),
        out_shape=(
            jax.ShapeDtypeStruct((tok * heads, width), f32),
            jax.ShapeDtypeStruct((BLOCK * heads, width), f32),
            jax.ShapeDtypeStruct((1, 1), f32),
        ),
        in_specs=[anywhere] * 5 + [in_smem],
        out_specs=(in_vmem, in_vmem, in_smem),
        scratch_shapes=[
            pltpu.VMEM((n, 2, tok, width), bf16),
            pltpu.VMEM((tok * heads, width), bf16),
            pltpu.VMEM(feat_q.shape, bf16),
            pltpu.VMEM(feat_k.shape, bf16),
            pltpu.VMEM((heads * 128, width), bf16),
            pltpu.VMEM((tok * heads, width), f32),
            pltpu.VMEM((width, heads * BLOCK), bf16),
            pltpu.VMEM((heads, tok, 256), bf16),
            pltpu.VMEM((heads, 256, 2 * width), f32),
            pltpu.VMEM((heads, tok, width), f32),
            pltpu.VMEM((heads, tok, width), f32),
            pltpu.VMEM((1, heads * BLOCK), f32),
            pltpu.VMEM((1, heads * BLOCK), f32),
            pltpu.VMEM((width, heads * BLOCK), f32),
            pltpu.VMEM((8, width), f32),
            pltpu.VMEM((8, width), f32),
            pltpu.VMEM((2 * nh, 8, width), f32),
            pltpu.VMEM((8, width), f32),
            dma((5,)), dma((n, 2)), dma((2, n, 2)), dma((2,)), dma((2 * nh,)), dma((2 * nh,)), dma((n // 2,)), dma((1,)),
        ],
        compiler_params=pltpu.CompilerParams(
            collective_id=0, has_side_effects=True, vmem_limit_bytes=60 * 1024 * 1024
        ),
    )(
        queries.reshape(tok * heads, width), keys.reshape(tok, width), values.reshape(tok, width),
        feat_q, feat_k, samples,
    )
    return student.reshape(tok, heads, width).astype(bf16), teacher.reshape(1, BLOCK, heads, width), loss.reshape(())


def solution(mesh):
    in_specs = (
        P("seq", "head", None),
        P("seq", "head", None),
        P("seq", "head", None),
        P("head", None, None),
        P("head", None, None),
        P(),
    )
    out_specs = (P("seq", "head", None), P("seq", None, "head", None), P())
    return jax.shard_map(
        functools.partial(on_device, mesh.shape["seq"], mesh.shape["head"]),
        mesh=mesh, in_specs=in_specs, out_specs=out_specs, check_vma=False,
    )
```

```python
import functools

import jax
import jax.numpy as jnp
from jax import lax
from jax.experimental import pallas as pl
from jax.experimental.pallas import tpu as pltpu
from jax.sharding import PartitionSpec as P

BLOCK = 128
MASKED = -1e30
LOG2E = 1.4426950408889634
NT = (((1,), (1,)), ((), ()))


def dot(a, b):
    return jnp.dot(a, b, preferred_element_type=jnp.float32)


def soft_pair(logits, axis):
    up = jnp.exp(logits - jnp.max(logits, axis=axis, keepdims=True))
    down = jnp.exp(jnp.min(logits, axis=axis, keepdims=True) - logits)
    up = up * (1.0 / jnp.sum(up, axis=axis, keepdims=True))
    down = down * (1.0 / jnp.sum(down, axis=axis, keepdims=True))
    return jnp.concatenate([up, down], axis=axis)


def kernel(
    n, nh, q_hbm, k_hbm, v_hbm, fq_hbm, fk_hbm, samples_hbm, student, teacher, loss,
    samples, kv, q_raw, fq, fk, fk_t, rows32, qs_t, phi_q, phi_s, state, num, den, num_s, den_s, top, tot, acc, out32, column, below, plane, total,
    local_sem, recv_sem, send_sem, up_sem, plane_send, plane_recv, down_send, down_recv,
):
    tok, width = k_hbm.shape
    heads = fq.shape[0]
    s, hd = lax.axis_index("seq"), lax.axis_index("head")
    outer, y = s // 2, s % 2
    last = n // 2 - 1
    partner = s + 1 - 2 * y
    own = (k_hbm, v_hbm)

    local = [
        pltpu.make_async_copy(src, dst, local_sem.at[i])
        for i, (src, dst) in enumerate(
            [(q_hbm, q_raw), (fq_hbm, fq), (fk_hbm, fk), (k_hbm, kv.at[s, 0]), (v_hbm, kv.at[s, 1]),
             (samples_hbm, samples)]
        )
    ]
    for copy in local:
        copy.start()

    barrier = pltpu.get_barrier_semaphore()
    mate = y * nh + hd

    def plane_device(i):
        other = lax.rem(mate + i, 2 * nh)
        return {"seq": 2 * outer + other // nh, "head": lax.rem(other, nh)}

    for i in range(1, 2 * nh):
        pl.semaphore_signal(barrier, inc=1, device_id=plane_device(i), device_id_type=pl.DeviceIdType.MESH)

    @pl.when(outer > 0)
    def _():
        pl.semaphore_signal(barrier, inc=1, device_id={"seq": s - 2}, device_id_type=pl.DeviceIdType.MESH)

    @pl.when(outer < last)
    def _():
        pl.semaphore_signal(barrier, inc=1, device_id={"seq": s + 2}, device_id_type=pl.DeviceIdType.MESH)

    pl.semaphore_wait(barrier, 2 * nh - 1 + jnp.minimum(outer, 1) + jnp.minimum(last - outer, 1))

    def hop(src, slot, j, way, target):
        return pltpu.make_async_remote_copy(
            src_ref=src, dst_ref=kv.at[slot, j], send_sem=send_sem.at[way, slot, j],
            recv_sem=recv_sem.at[slot, j], device_id={"seq": target}, device_id_type=pl.DeviceIdType.MESH,
        )

    @pl.when(outer < last)
    def _():
        for j in range(2):
            hop(own[j], s, j, 0, s + 2).start()

    @pl.when(y == 0)
    def _():
        for j in range(2):
            hop(own[j], s, j, 1, partner).start()


    def chosen(rows):
        block = rows[:BLOCK]
        for b in range(1, tok // BLOCK):
            block = jnp.where(pick == b, rows[b * BLOCK:(b + 1) * BLOCK], block)
        return block

    def key_features(keys, h):
        logits = lax.dot_general(fk_t[h * 128:(h + 1) * 128, :], keys, NT, preferred_element_type=jnp.float32)
        return soft_pair(logits, 0).astype(jnp.bfloat16)

    def weigh(keys, live):
        out = []
        for c in range(heads // 2):
            cols = slice(c * 2 * BLOCK, (c + 1) * 2 * BLOCK)
            scores = dot(keys, qs_t[:, cols]) * (LOG2E / width ** 0.5)
            if live is not None:
                scores = jnp.where(live, scores, MASKED)
            peak = jnp.max(scores, axis=0, keepdims=True)
            fade = None
            if live is None:
                old = top[:, cols]
                peak = jnp.maximum(old, peak)
                fade = jnp.exp2(old - peak)
            weights = jnp.exp2(scores - peak)
            part = jnp.sum(weights, axis=0, keepdims=True)
            top[:, cols] = peak
            tot[:, cols] = part if live is not None else part + tot[:, cols] * fade
            out.append((cols, weights.astype(jnp.bfloat16), fade))
        return out

    def mix(weighed, values):
        values_t = values.astype(jnp.float32).T.astype(jnp.bfloat16)
        for cols, weights, fade in weighed:
            mixed = dot(values_t, weights)
            acc[:, cols] = mixed if fade is None else mixed + acc[:, cols] * fade

    def arrived(slot, j):
        hop(kv.at[slot, j], slot, j, 0, partner).wait_recv()

    def absorb(slot, wait):
        if wait:
            arrived(slot, 0)
        keys = kv[slot, 0]
        weighed = weigh(keys, None)
        features = [key_features(keys, h) for h in range(heads)]
        if wait:
            arrived(slot, 1)
        values = kv[slot, 1]
        mix(weighed, values)
        values_wide = jnp.concatenate([values, jnp.ones_like(values)], axis=1)
        for h in range(heads):
            state[h] += dot(features[h], values_wide)

    def relay(slot):
        for j in range(2):
            arrived(slot, j)

            @pl.when(outer < last)
            def _():
                hop(kv.at[slot, j], slot, j, 0, s + 2).start()

            hop(kv.at[slot, j], slot, j, 1, partner).start()

    state[...] = jnp.zeros_like(state)
    for copy in local:
        copy.wait()
    pick = samples[s]
    rows32[...] = q_raw[...].astype(jnp.float32)
    for h in range(heads):
        mine = rows32[pl.ds(h, tok, stride=heads), :]
        qs_t[:, h * BLOCK:(h + 1) * BLOCK] = chosen(mine).T.astype(jnp.bfloat16)
        fk_t[h * 128:(h + 1) * 128, :] = fk[h].astype(jnp.float32).T.astype(jnp.bfloat16)
        phi = soft_pair(dot(mine.astype(jnp.bfloat16), fq[h]), 1)
        phi_q[h] = phi.astype(jnp.bfloat16)
        phi_s[h] = chosen(phi).astype(jnp.bfloat16)

    @pl.when(outer > 0)
    def _():
        relay(s - 2)

    keys, values = kv[s, 0], kv[s, 1]
    place = lax.broadcasted_iota(jnp.int32, (tok, 2 * BLOCK), 0)
    row = lax.broadcasted_iota(jnp.int32, (tok, 2 * BLOCK), 1) % BLOCK + pick * BLOCK
    mix(weigh(keys, place <= row), values)

    @pl.when(outer > 1)
    def _():
        relay(s - 4)

    causal = lax.broadcasted_iota(jnp.int32, (tok, tok), 0) >= lax.broadcasted_iota(jnp.int32, (tok, tok), 1)
    for h in range(heads):
        inner = jnp.where(causal, dot(phi_q[h], key_features(keys, h)), 0.0)
        num[h] = dot(inner.astype(jnp.bfloat16), values)
        den[h] = jnp.broadcast_to(jnp.sum(inner, axis=1, keepdims=True), (tok, width))
        num_s[h] = chosen(num[h])
        den_s[h] = chosen(den[h])

    @pl.when(y == 1)
    def _():
        absorb(partner, True)

    def lap(d, carry):
        absorb(s - 2 * d, False)

        @pl.when(d + 2 <= outer)
        def _():
            relay(s - 2 * d - 4)

        absorb(partner - 2 * d, True)
        return carry

    lax.fori_loop(1, outer + 1, lap, 0)

    def finish(h, phi, numer, denom):
        inter = dot(phi[h], state[h].astype(jnp.bfloat16))
        result = (numer[h] + inter[:, :width]) / (denom[h] + inter[:, width:])
        return result.astype(jnp.bfloat16).astype(jnp.float32)

    part = jnp.zeros((8, width), jnp.float32)
    for h in range(heads):
        cols = slice(h * BLOCK, (h + 1) * BLOCK)
        mixed = (acc[:, cols] / tot[:, cols]).T
        teacher[pl.ds(h, BLOCK, stride=heads), :] = mixed
        gap = finish(h, phi_s, num_s, den_s) - mixed
        part = part + jnp.sum((gap * gap).reshape(BLOCK // 8, 8, width), axis=0)

    def send(src, dst, send_sem, recv_sem, device):
        return pltpu.make_async_remote_copy(
            src_ref=src, dst_ref=dst, send_sem=send_sem, recv_sem=recv_sem,
            device_id=device, device_id_type=pl.DeviceIdType.MESH,
        )

    upward = send(column, below, up_sem.at[0], up_sem.at[1], {"seq": s + 2})
    across = [
        send(plane.at[mate], plane.at[mate], plane_send.at[i], plane_recv.at[i], plane_device(i))
        for i in range(1, 2 * nh)
    ]
    downward = [
        send(total, total, down_send.at[i], down_recv.at[0], {"seq": s - 2 * i}) for i in range(1, last + 1)
    ]
    column[...] = part

    @pl.when(outer > 0)
    def _():
        upward.wait_recv()
        column[...] += below[...]

    @pl.when(outer < last)
    def _():
        upward.start()

    @pl.when(outer == last)
    def _():
        plane[mate] = column[...]
        for copy in across:
            copy.start()

    for h in range(heads):
        out32[pl.ds(h, tok, stride=heads), :] = finish(h, phi_q, num, den)

    @pl.when(outer == last)
    def _():
        for copy in across:
            copy.wait()
        total[...] = jnp.sum(plane[...], axis=0)
        for copy in downward:
            copy.start()

    student[...] = out32[...].astype(jnp.bfloat16)

    @pl.when(outer < last)
    def _():
        for j in range(2):
            hop(own[j], s, j, 0, s + 2).wait_send()

    @pl.when(y == 0)
    def _():
        for j in range(2):
            hop(own[j], s, j, 1, partner).wait_send()

    def drain(d, carry):
        near = s - 2 * d
        for j in range(2):
            @pl.when(outer < last)
            def _():
                hop(kv.at[near, j], near, j, 0, s + 2).wait_send()

            hop(kv.at[near, j], near, j, 1, partner).wait_send()
        return carry

    lax.fori_loop(1, outer + 1, drain, 0)

    @pl.when(outer == last)
    def _():
        for copy in downward:
            copy.wait_send()

    @pl.when(outer < last)
    def _():
        upward.wait_send()
        downward[0].wait_recv()

    loss[0, 0] = jnp.sum(total[...]) * (1.0 / (n * nh * BLOCK * heads * width))


def on_device(n, nh, queries, keys, values, feat_q, feat_k, samples):
    tok, heads, width = queries.shape
    bf16, f32 = jnp.bfloat16, jnp.float32
    in_hbm = pl.BlockSpec(memory_space=pltpu.HBM)
    in_vmem = pl.BlockSpec(memory_space=pltpu.VMEM)
    in_smem = pl.BlockSpec(memory_space=pltpu.SMEM)
    dma = pltpu.SemaphoreType.DMA
    student, teacher, loss = pl.pallas_call(
        functools.partial(kernel, n, nh),
        out_shape=(
            jax.ShapeDtypeStruct((tok * heads, width), bf16),
            jax.ShapeDtypeStruct((BLOCK * heads, width), f32),
            jax.ShapeDtypeStruct((1, 1), f32),
        ),
        in_specs=[in_hbm] * 6,
        out_specs=(in_vmem, in_vmem, in_smem),
        scratch_shapes=[
            pltpu.SMEM((n,), jnp.int32),
            pltpu.VMEM((n, 2, tok, width), bf16),
            pltpu.VMEM((tok * heads, width), bf16),
            pltpu.VMEM(feat_q.shape, bf16),
            pltpu.VMEM(feat_k.shape, bf16),
            pltpu.VMEM((heads * 128, width), bf16),
            pltpu.VMEM((tok * heads, width), f32),
            pltpu.VMEM((width, heads * BLOCK), bf16),
            pltpu.VMEM((heads, tok, 256), bf16),
            pltpu.VMEM((heads, BLOCK, 256), bf16),
            pltpu.VMEM((heads, 256, 2 * width), f32),
            pltpu.VMEM((heads, tok, width), f32),
            pltpu.VMEM((heads, tok, width), f32),
            pltpu.VMEM((heads, BLOCK, width), f32),
            pltpu.VMEM((heads, BLOCK, width), f32),
            pltpu.VMEM((1, heads * BLOCK), f32),
            pltpu.VMEM((1, heads * BLOCK), f32),
            pltpu.VMEM((width, heads * BLOCK), f32),
            pltpu.VMEM((tok * heads, width), f32),
            pltpu.VMEM((8, width), f32),
            pltpu.VMEM((8, width), f32),
            pltpu.VMEM((2 * nh, 8, width), f32),
            pltpu.VMEM((8, width), f32),
            dma((6,)), dma((n, 2)), dma((2, n, 2)), dma((2,)), dma((2 * nh,)), dma((2 * nh,)), dma((n // 2,)), dma((1,)),
        ],
        compiler_params=pltpu.CompilerParams(
            collective_id=0, has_side_effects=True, vmem_limit_bytes=24 * 1024 * 1024
        ),
    )(*(
        pltpu.with_memory_space_constraint(x, pltpu.HBM) for x in (
            queries.reshape(tok * heads, width), keys.reshape(tok, width), values.reshape(tok, width), feat_q, feat_k, samples,
        )
    ))
    return student.reshape(tok, heads, width), teacher.reshape(1, BLOCK, heads, width), loss.reshape(())


def solution(mesh):
    in_specs = (
        P("seq", "head", None),
        P("seq", "head", None),
        P("seq", "head", None),
        P("head", None, None),
        P("head", None, None),
        P(),
    )
    out_specs = (P("seq", "head", None), P("seq", None, "head", None), P())
    return jax.shard_map(
        functools.partial(on_device, mesh.shape["seq"], mesh.shape["head"]),
        mesh=mesh, in_specs=in_specs, out_specs=out_specs, check_vma=False,
    )
```

```python
import functools

import jax
import jax.numpy as jnp
from jax import lax
from jax.experimental import pallas as pl
from jax.experimental.pallas import tpu as pltpu
from jax.sharding import PartitionSpec as P

BLOCK = 128
MASKED = -1e30
LOG2E = 1.4426950408889634
NT = (((1,), (1,)), ((), ()))


def dot(a, b):
    return jnp.dot(a, b, preferred_element_type=jnp.float32)


def soft_pair(logits, axis):
    logits = logits * LOG2E
    up = jnp.exp2(logits - jnp.max(logits, axis=axis, keepdims=True))
    down = jnp.exp2(jnp.min(logits, axis=axis, keepdims=True) - logits)
    up = up * (1.0 / jnp.sum(up, axis=axis, keepdims=True))
    down = down * (1.0 / jnp.sum(down, axis=axis, keepdims=True))
    return jnp.concatenate([up, down], axis=axis)


def kernel(
    n, nh, q_hbm, k_hbm, v_hbm, fq_hbm, fk_hbm, samples_hbm, student, teacher, loss,
    samples, kv, q_raw, fq, fk, fk_t, rows32, qs_t, phi_q, phi_s, feats, state, state_low, num, den, num_s, den_s, top, tot, acc, out32, column, below, plane, total,
    local_sem, recv_sem, send_sem, up_sem, plane_send, plane_recv, down_send, down_recv,
):
    tok, width = k_hbm.shape
    heads = fq.shape[0]
    s, hd = lax.axis_index("seq"), lax.axis_index("head")
    outer, y = s // 2, s % 2
    last = n // 2 - 1
    partner = s + 1 - 2 * y
    own = (k_hbm, v_hbm)

    local = [
        pltpu.make_async_copy(src, dst, local_sem.at[i])
        for i, (src, dst) in enumerate(
            [(q_hbm, q_raw), (fq_hbm, fq), (fk_hbm, fk), (k_hbm, kv.at[s, 0]), (v_hbm, kv.at[s, 1]),
             (samples_hbm, samples)]
        )
    ]
    for copy in local:
        copy.start()

    barrier = pltpu.get_barrier_semaphore()
    mate = y * nh + hd

    def plane_device(i):
        other = lax.rem(mate + i, 2 * nh)
        return {"seq": 2 * outer + other // nh, "head": lax.rem(other, nh)}

    for i in range(1, 2 * nh):
        pl.semaphore_signal(barrier, inc=1, device_id=plane_device(i), device_id_type=pl.DeviceIdType.MESH)

    @pl.when(outer > 0)
    def _():
        pl.semaphore_signal(barrier, inc=1, device_id={"seq": s - 2}, device_id_type=pl.DeviceIdType.MESH)

    @pl.when(outer < last)
    def _():
        pl.semaphore_signal(barrier, inc=1, device_id={"seq": s + 2}, device_id_type=pl.DeviceIdType.MESH)

    pl.semaphore_wait(barrier, 2 * nh - 1 + jnp.minimum(outer, 1) + jnp.minimum(last - outer, 1))

    def hop(src, slot, j, way, target):
        return pltpu.make_async_remote_copy(
            src_ref=src, dst_ref=kv.at[slot, j], send_sem=send_sem.at[way, slot, j],
            recv_sem=recv_sem.at[slot, j], device_id={"seq": target}, device_id_type=pl.DeviceIdType.MESH,
        )

    @pl.when(outer < last)
    def _():
        for j in range(2):
            hop(own[j], s, j, 0, s + 2).start()

    @pl.when(y == 0)
    def _():
        for j in range(2):
            hop(own[j], s, j, 1, partner).start()


    def chosen(rows):
        block = rows[:BLOCK]
        for b in range(1, tok // BLOCK):
            block = jnp.where(pick == b, rows[b * BLOCK:(b + 1) * BLOCK], block)
        return block

    def key_features(keys):
        logits = lax.dot_general(fk_t[...], keys, NT, preferred_element_type=jnp.float32)
        for h in range(heads):
            feats[h * 256:(h + 1) * 256, :] = soft_pair(logits[h * 128:(h + 1) * 128], 0).astype(jnp.bfloat16)

    def weigh(keys, live):
        out = []
        for c in range(heads // 2):
            cols = slice(c * 2 * BLOCK, (c + 1) * 2 * BLOCK)
            scores = dot(keys, qs_t[:, cols]) * (LOG2E / width ** 0.5)
            if live is not None:
                scores = jnp.where(live, scores, MASKED)
            peak = jnp.max(scores, axis=0, keepdims=True)
            fade = None
            if live is None:
                old = top[:, cols]
                peak = jnp.maximum(old, peak)
                fade = jnp.exp2(old - peak)
            weights = jnp.exp2(scores - peak)
            part = jnp.sum(weights, axis=0, keepdims=True)
            top[:, cols] = peak
            tot[:, cols] = part if live is not None else part + tot[:, cols] * fade
            out.append((cols, weights.astype(jnp.bfloat16), fade))
        return out

    def mix(weighed, values):
        values_t = values.astype(jnp.float32).T.astype(jnp.bfloat16)
        for cols, weights, fade in weighed:
            mixed = dot(values_t, weights)
            acc[:, cols] = mixed if fade is None else mixed + acc[:, cols] * fade

    def arrived(slot, j):
        hop(kv.at[slot, j], slot, j, 0, partner).wait_recv()

    def absorb(slot, wait):
        if wait:
            arrived(slot, 0)
        keys = kv[slot, 0]
        weighed = weigh(keys, None)
        key_features(keys)
        if wait:
            arrived(slot, 1)
        values = kv[slot, 1]
        mix(weighed, values)
        values_wide = jnp.concatenate([values, jnp.ones_like(values)], axis=1)
        state[...] += dot(feats[...], values_wide)

    def relay(slot):
        for j in range(2):
            arrived(slot, j)

            @pl.when(outer < last)
            def _():
                hop(kv.at[slot, j], slot, j, 0, s + 2).start()

            hop(kv.at[slot, j], slot, j, 1, partner).start()

    state[...] = jnp.zeros_like(state)
    for copy in local:
        copy.wait()
    pick = samples[s]
    rows32[...] = q_raw[...].astype(jnp.float32)
    for h in range(heads):
        mine = rows32[pl.ds(h, tok, stride=heads), :]
        qs_t[:, h * BLOCK:(h + 1) * BLOCK] = chosen(mine).T.astype(jnp.bfloat16)
        fk_t[h * 128:(h + 1) * 128, :] = fk[h].astype(jnp.float32).T.astype(jnp.bfloat16)
        phi = soft_pair(dot(mine.astype(jnp.bfloat16), fq[h]), 1)
        phi_q[h] = phi.astype(jnp.bfloat16)
        phi_s[h] = chosen(phi).astype(jnp.bfloat16)

    @pl.when(outer > 0)
    def _():
        relay(s - 2)

    keys, values = kv[s, 0], kv[s, 1]
    place = lax.broadcasted_iota(jnp.int32, (tok, 2 * BLOCK), 0)
    row = lax.broadcasted_iota(jnp.int32, (tok, 2 * BLOCK), 1) % BLOCK + pick * BLOCK
    mix(weigh(keys, place <= row), values)

    @pl.when(outer > 1)
    def _():
        relay(s - 4)

    causal = lax.broadcasted_iota(jnp.int32, (tok, tok), 0) >= lax.broadcasted_iota(jnp.int32, (tok, tok), 1)
    key_features(keys)
    for h in range(heads):
        inner = jnp.where(causal, dot(phi_q[h], feats[h * 256:(h + 1) * 256, :]), 0.0)
        num[h] = dot(inner.astype(jnp.bfloat16), values)
        den[h] = jnp.broadcast_to(jnp.sum(inner, axis=1, keepdims=True), (tok, width))
        num_s[h] = chosen(num[h])
        den_s[h] = chosen(den[h])

    @pl.when(y == 1)
    def _():
        absorb(partner, True)

    def lap(d, carry):
        absorb(s - 2 * d, False)

        @pl.when(d + 2 <= outer)
        def _():
            relay(s - 2 * d - 4)

        absorb(partner - 2 * d, True)
        return carry

    lax.fori_loop(1, outer + 1, lap, 0)

    def finish(h, phi, numer, denom):
        inter = dot(phi[h], state_low[h * 256:(h + 1) * 256, :])
        result = (numer[h] + inter[:, :width]) / (denom[h] + inter[:, width:])
        return result.astype(jnp.bfloat16).astype(jnp.float32)

    state_low[...] = state[...].astype(jnp.bfloat16)
    part = jnp.zeros((8, width), jnp.float32)
    for h in range(heads):
        cols = slice(h * BLOCK, (h + 1) * BLOCK)
        mixed = (acc[:, cols] / tot[:, cols]).T
        teacher[pl.ds(h, BLOCK, stride=heads), :] = mixed
        gap = finish(h, phi_s, num_s, den_s) - mixed
        part = part + jnp.sum((gap * gap).reshape(BLOCK // 8, 8, width), axis=0)

    def send(src, dst, send_sem, recv_sem, device):
        return pltpu.make_async_remote_copy(
            src_ref=src, dst_ref=dst, send_sem=send_sem, recv_sem=recv_sem,
            device_id=device, device_id_type=pl.DeviceIdType.MESH,
        )

    upward = send(column, below, up_sem.at[0], up_sem.at[1], {"seq": s + 2})
    across = [
        send(plane.at[mate], plane.at[mate], plane_send.at[i], plane_recv.at[i], plane_device(i))
        for i in range(1, 2 * nh)
    ]
    downward = [
        send(total, total, down_send.at[i], down_recv.at[0], {"seq": s - 2 * i}) for i in range(1, last + 1)
    ]
    column[...] = part

    @pl.when(outer > 0)
    def _():
        upward.wait_recv()
        column[...] += below[...]

    @pl.when(outer < last)
    def _():
        upward.start()

    @pl.when(outer == last)
    def _():
        plane[mate] = column[...]
        for copy in across:
            copy.start()

    for h in range(heads):
        out32[pl.ds(h, tok, stride=heads), :] = finish(h, phi_q, num, den)

    @pl.when(outer == last)
    def _():
        for copy in across:
            copy.wait()
        total[...] = jnp.sum(plane[...], axis=0)
        for copy in downward:
            copy.start()

    student[...] = out32[...].astype(jnp.bfloat16)

    @pl.when(outer < last)
    def _():
        for j in range(2):
            hop(own[j], s, j, 0, s + 2).wait_send()

    @pl.when(y == 0)
    def _():
        for j in range(2):
            hop(own[j], s, j, 1, partner).wait_send()

    def drain(d, carry):
        near = s - 2 * d
        for j in range(2):
            @pl.when(outer < last)
            def _():
                hop(kv.at[near, j], near, j, 0, s + 2).wait_send()

            hop(kv.at[near, j], near, j, 1, partner).wait_send()
        return carry

    lax.fori_loop(1, outer + 1, drain, 0)

    @pl.when(outer == last)
    def _():
        for copy in downward:
            copy.wait_send()

    @pl.when(outer < last)
    def _():
        upward.wait_send()
        downward[0].wait_recv()

    loss[0, 0] = jnp.sum(total[...]) * (1.0 / (n * nh * BLOCK * heads * width))


def on_device(n, nh, queries, keys, values, feat_q, feat_k, samples):
    tok, heads, width = queries.shape
    bf16, f32 = jnp.bfloat16, jnp.float32
    in_hbm = pl.BlockSpec(memory_space=pltpu.HBM)
    in_vmem = pl.BlockSpec(memory_space=pltpu.VMEM)
    in_smem = pl.BlockSpec(memory_space=pltpu.SMEM)
    dma = pltpu.SemaphoreType.DMA
    student, teacher, loss = pl.pallas_call(
        functools.partial(kernel, n, nh),
        out_shape=(
            jax.ShapeDtypeStruct((tok * heads, width), bf16),
            jax.ShapeDtypeStruct((BLOCK * heads, width), f32),
            jax.ShapeDtypeStruct((1, 1), f32),
        ),
        in_specs=[in_hbm] * 6,
        out_specs=(in_vmem, in_vmem, in_smem),
        scratch_shapes=[
            pltpu.SMEM((n,), jnp.int32),
            pltpu.VMEM((n, 2, tok, width), bf16),
            pltpu.VMEM((tok * heads, width), bf16),
            pltpu.VMEM(feat_q.shape, bf16),
            pltpu.VMEM(feat_k.shape, bf16),
            pltpu.VMEM((heads * 128, width), bf16),
            pltpu.VMEM((tok * heads, width), f32),
            pltpu.VMEM((width, heads * BLOCK), bf16),
            pltpu.VMEM((heads, tok, 256), bf16),
            pltpu.VMEM((heads, BLOCK, 256), bf16),
            pltpu.VMEM((heads * 256, tok), bf16),
            pltpu.VMEM((heads * 256, 2 * width), f32),
            pltpu.VMEM((heads * 256, 2 * width), bf16),
            pltpu.VMEM((heads, tok, width), f32),
            pltpu.VMEM((heads, tok, width), f32),
            pltpu.VMEM((heads, BLOCK, width), f32),
            pltpu.VMEM((heads, BLOCK, width), f32),
            pltpu.VMEM((1, heads * BLOCK), f32),
            pltpu.VMEM((1, heads * BLOCK), f32),
            pltpu.VMEM((width, heads * BLOCK), f32),
            pltpu.VMEM((tok * heads, width), f32),
            pltpu.VMEM((8, width), f32),
            pltpu.VMEM((8, width), f32),
            pltpu.VMEM((2 * nh, 8, width), f32),
            pltpu.VMEM((8, width), f32),
            dma((6,)), dma((n, 2)), dma((2, n, 2)), dma((2,)), dma((2 * nh,)), dma((2 * nh,)), dma((n // 2,)), dma((1,)),
        ],
        compiler_params=pltpu.CompilerParams(
            collective_id=0, has_side_effects=True, vmem_limit_bytes=24 * 1024 * 1024
        ),
    )(*(
        pltpu.with_memory_space_constraint(x, pltpu.HBM) for x in (
            queries.reshape(tok * heads, width), keys.reshape(tok, width), values.reshape(tok, width), feat_q, feat_k, samples,
        )
    ))
    return student.reshape(tok, heads, width), teacher.reshape(1, BLOCK, heads, width), loss.reshape(())


def solution(mesh):
    in_specs = (
        P("seq", "head", None),
        P("seq", "head", None),
        P("seq", "head", None),
        P("head", None, None),
        P("head", None, None),
        P(),
    )
    out_specs = (P("seq", "head", None), P("seq", None, "head", None), P())
    return jax.shard_map(
        functools.partial(on_device, mesh.shape["seq"], mesh.shape["head"]),
        mesh=mesh, in_specs=in_specs, out_specs=out_specs, check_vma=False,
    )
```

```python
import functools

import jax
import jax.numpy as jnp
from jax import lax
from jax.experimental import pallas as pl
from jax.experimental.pallas import tpu as pltpu
from jax.sharding import PartitionSpec as P

BLOCK = 128
MASKED = -1e30
LOG2E = 1.4426950408889634
NT = (((1,), (1,)), ((), ()))


def dot(a, b):
    return jnp.dot(a, b, preferred_element_type=jnp.float32)


def soft_pair(logits, axis):
    logits = logits * LOG2E
    up = jnp.exp2(logits - jnp.max(logits, axis=axis, keepdims=True))
    down = jnp.exp2(jnp.min(logits, axis=axis, keepdims=True) - logits)
    up = up * (1.0 / jnp.sum(up, axis=axis, keepdims=True))
    down = down * (1.0 / jnp.sum(down, axis=axis, keepdims=True))
    return jnp.concatenate([up, down], axis=axis)


def kernel(
    n, nh, q_hbm, k_hbm, v_hbm, fq_hbm, fk_hbm, samples_hbm, student, teacher, loss,
    samples, kv, q_raw, fq, fk, fk_t, rows32, qs_t, phi_q, phi_s, feats, state, state_low, num, den, num_s, den_s, top, tot, acc, out32, column, below, plane, total,
    local_sem, recv_sem, send_sem, up_sem, plane_send, plane_recv, down_send, down_recv,
):
    tok, width = k_hbm.shape
    heads = fq.shape[0]
    s, hd = lax.axis_index("seq"), lax.axis_index("head")
    outer, y = s // 2, s % 2
    last = n // 2 - 1
    partner = s + 1 - 2 * y
    own = (k_hbm, v_hbm)

    local = [
        pltpu.make_async_copy(src, dst, local_sem.at[i])
        for i, (src, dst) in enumerate(
            [(q_hbm, q_raw), (fq_hbm, fq), (fk_hbm, fk), (k_hbm, kv.at[s, 0]), (v_hbm, kv.at[s, 1]),
             (samples_hbm, samples)]
        )
    ]
    for copy in local:
        copy.start()

    barrier = pltpu.get_barrier_semaphore()
    mate = y * nh + hd

    def plane_device(i):
        other = lax.rem(mate + i, 2 * nh)
        return {"seq": 2 * outer + other // nh, "head": lax.rem(other, nh)}

    for i in range(1, 2 * nh):
        pl.semaphore_signal(barrier, inc=1, device_id=plane_device(i), device_id_type=pl.DeviceIdType.MESH)

    @pl.when(outer > 0)
    def _():
        pl.semaphore_signal(barrier, inc=1, device_id={"seq": s - 2}, device_id_type=pl.DeviceIdType.MESH)

    @pl.when(outer < last)
    def _():
        pl.semaphore_signal(barrier, inc=1, device_id={"seq": s + 2}, device_id_type=pl.DeviceIdType.MESH)

    pl.semaphore_wait(barrier, 2 * nh - 1 + jnp.minimum(outer, 1) + jnp.minimum(last - outer, 1))

    def hop(src, slot, j, way, target):
        return pltpu.make_async_remote_copy(
            src_ref=src, dst_ref=kv.at[slot, j], send_sem=send_sem.at[way, slot, j],
            recv_sem=recv_sem.at[slot, j], device_id={"seq": target}, device_id_type=pl.DeviceIdType.MESH,
        )

    @pl.when(outer < last)
    def _():
        for j in range(2):
            hop(own[j], s, j, 0, s + 2).start()

    @pl.when(y == 0)
    def _():
        for j in range(2):
            hop(own[j], s, j, 1, partner).start()


    def chosen(rows):
        block = rows[:BLOCK]
        for b in range(1, tok // BLOCK):
            block = jnp.where(pick == b, rows[b * BLOCK:(b + 1) * BLOCK], block)
        return block

    def key_features(keys):
        logits = lax.dot_general(fk_t[...], keys, NT, preferred_element_type=jnp.float32)
        for h in range(heads):
            feats[h * 256:(h + 1) * 256, :] = soft_pair(logits[h * 128:(h + 1) * 128], 0).astype(jnp.bfloat16)

    def weigh(keys, live):
        out = []
        for c in range(heads // 2):
            cols = slice(c * 2 * BLOCK, (c + 1) * 2 * BLOCK)
            scores = dot(keys, qs_t[:, cols]) * (LOG2E / width ** 0.5)
            if live is not None:
                scores = jnp.where(live, scores, MASKED)
            peak = jnp.max(scores, axis=0, keepdims=True)
            fade = None
            if live is None:
                old = top[:, cols]
                peak = jnp.maximum(old, peak)
                fade = jnp.exp2(old - peak)
            weights = jnp.exp2(scores - peak)
            part = jnp.sum(weights, axis=0, keepdims=True)
            top[:, cols] = peak
            tot[:, cols] = part if live is not None else part + tot[:, cols] * fade
            out.append((cols, weights.astype(jnp.bfloat16), fade))
        return out

    def mix(weighed, values):
        values_t = values.astype(jnp.float32).T.astype(jnp.bfloat16)
        for cols, weights, fade in weighed:
            mixed = dot(values_t, weights)
            acc[:, cols] = mixed if fade is None else mixed + acc[:, cols] * fade

    def arrived(slot, j):
        hop(kv.at[slot, j], slot, j, 0, partner).wait_recv()

    def absorb(slot, wait):
        if wait:
            arrived(slot, 0)
        keys = kv[slot, 0]
        weighed = weigh(keys, None)
        key_features(keys)
        if wait:
            arrived(slot, 1)
        values = kv[slot, 1]
        mix(weighed, values)
        values_wide = jnp.concatenate([values, jnp.ones_like(values)], axis=1)
        state[...] += dot(feats[...], values_wide)

    def relay(d, j):
        @pl.when(d <= outer)
        def _():
            slot = s - 2 * d
            arrived(slot, j)

            @pl.when(outer < last)
            def _():
                hop(kv.at[slot, j], slot, j, 0, s + 2).start()

            hop(kv.at[slot, j], slot, j, 1, partner).start()

    state[...] = jnp.zeros_like(state)
    for copy in local:
        copy.wait()
    pick = samples[s]
    rows32[...] = q_raw[...].astype(jnp.float32)
    for h in range(heads):
        qs_t[:, h * BLOCK:(h + 1) * BLOCK] = chosen(rows32[pl.ds(h, tok, stride=heads), :]).T.astype(jnp.bfloat16)
        fk_t[h * 128:(h + 1) * 128, :] = fk[h].astype(jnp.float32).T.astype(jnp.bfloat16)

    relay(1, 0)
    for h in range(heads):
        mine = rows32[pl.ds(h, tok, stride=heads), :]
        phi = soft_pair(dot(mine.astype(jnp.bfloat16), fq[h]), 1)
        phi_q[h] = phi.astype(jnp.bfloat16)
        phi_s[h] = chosen(phi).astype(jnp.bfloat16)
        if h == heads // 2 - 1:
            relay(1, 1)
    relay(2, 0)

    keys, values = kv[s, 0], kv[s, 1]
    place = lax.broadcasted_iota(jnp.int32, (tok, 2 * BLOCK), 0)
    row = lax.broadcasted_iota(jnp.int32, (tok, 2 * BLOCK), 1) % BLOCK + pick * BLOCK
    mix(weigh(keys, place <= row), values)

    relay(2, 1)

    causal = lax.broadcasted_iota(jnp.int32, (tok, tok), 0) >= lax.broadcasted_iota(jnp.int32, (tok, tok), 1)
    key_features(keys)
    for h in range(heads):
        inner = jnp.where(causal, dot(phi_q[h], feats[h * 256:(h + 1) * 256, :]), 0.0)
        num[h] = dot(inner.astype(jnp.bfloat16), values)
        den[h] = jnp.broadcast_to(jnp.sum(inner, axis=1, keepdims=True), (tok, width))
        num_s[h] = chosen(num[h])
        den_s[h] = chosen(den[h])

    @pl.when(y == 1)
    def _():
        absorb(partner, True)

    def lap(d, carry):
        absorb(s - 2 * d, False)

        relay(d + 2, 0)
        absorb(partner - 2 * d, True)
        relay(d + 2, 1)
        return carry

    lax.fori_loop(1, outer + 1, lap, 0)

    def finish(h, phi, numer, denom):
        inter = dot(phi[h], state_low[h * 256:(h + 1) * 256, :])
        result = (numer[h] + inter[:, :width]) / (denom[h] + inter[:, width:])
        return result.astype(jnp.bfloat16).astype(jnp.float32)

    state_low[...] = state[...].astype(jnp.bfloat16)
    part = jnp.zeros((8, width), jnp.float32)
    for h in range(heads):
        cols = slice(h * BLOCK, (h + 1) * BLOCK)
        mixed = (acc[:, cols] / tot[:, cols]).T
        teacher[pl.ds(h, BLOCK, stride=heads), :] = mixed
        gap = finish(h, phi_s, num_s, den_s) - mixed
        part = part + jnp.sum((gap * gap).reshape(BLOCK // 8, 8, width), axis=0)

    def send(src, dst, send_sem, recv_sem, device):
        return pltpu.make_async_remote_copy(
            src_ref=src, dst_ref=dst, send_sem=send_sem, recv_sem=recv_sem,
            device_id=device, device_id_type=pl.DeviceIdType.MESH,
        )

    upward = send(column, below, up_sem.at[0], up_sem.at[1], {"seq": s + 2})
    across = [
        send(plane.at[mate], plane.at[mate], plane_send.at[i], plane_recv.at[i], plane_device(i))
        for i in range(1, 2 * nh)
    ]
    downward = [
        send(total, total, down_send.at[i], down_recv.at[0], {"seq": s - 2 * i}) for i in range(1, last + 1)
    ]
    column[...] = part

    @pl.when(outer > 0)
    def _():
        upward.wait_recv()
        column[...] += below[...]

    @pl.when(outer < last)
    def _():
        upward.start()

    @pl.when(outer == last)
    def _():
        plane[mate] = column[...]
        for copy in across:
            copy.start()

    @pl.when(outer == last)
    def _():
        for copy in across:
            copy.wait()
        total[...] = jnp.sum(plane[...], axis=0)
        for copy in downward:
            copy.start()

    for h in range(heads):
        out32[pl.ds(h, tok, stride=heads), :] = finish(h, phi_q, num, den)
    student[...] = out32[...].astype(jnp.bfloat16)

    @pl.when(outer < last)
    def _():
        for j in range(2):
            hop(own[j], s, j, 0, s + 2).wait_send()

    @pl.when(y == 0)
    def _():
        for j in range(2):
            hop(own[j], s, j, 1, partner).wait_send()

    def drain(d, carry):
        near = s - 2 * d
        for j in range(2):
            @pl.when(outer < last)
            def _():
                hop(kv.at[near, j], near, j, 0, s + 2).wait_send()

            hop(kv.at[near, j], near, j, 1, partner).wait_send()
        return carry

    lax.fori_loop(1, outer + 1, drain, 0)

    @pl.when(outer == last)
    def _():
        for copy in downward:
            copy.wait_send()

    @pl.when(outer < last)
    def _():
        upward.wait_send()
        downward[0].wait_recv()

    loss[0, 0] = jnp.sum(total[...]) * (1.0 / (n * nh * BLOCK * heads * width))


def on_device(n, nh, queries, keys, values, feat_q, feat_k, samples):
    tok, heads, width = queries.shape
    bf16, f32 = jnp.bfloat16, jnp.float32
    in_hbm = pl.BlockSpec(memory_space=pltpu.HBM)
    in_vmem = pl.BlockSpec(memory_space=pltpu.VMEM)
    in_smem = pl.BlockSpec(memory_space=pltpu.SMEM)
    dma = pltpu.SemaphoreType.DMA
    student, teacher, loss = pl.pallas_call(
        functools.partial(kernel, n, nh),
        out_shape=(
            jax.ShapeDtypeStruct((tok * heads, width), bf16),
            jax.ShapeDtypeStruct((BLOCK * heads, width), f32),
            jax.ShapeDtypeStruct((1, 1), f32),
        ),
        in_specs=[in_hbm] * 6,
        out_specs=(in_vmem, in_vmem, in_smem),
        scratch_shapes=[
            pltpu.SMEM((n,), jnp.int32),
            pltpu.VMEM((n, 2, tok, width), bf16),
            pltpu.VMEM((tok * heads, width), bf16),
            pltpu.VMEM(feat_q.shape, bf16),
            pltpu.VMEM(feat_k.shape, bf16),
            pltpu.VMEM((heads * 128, width), bf16),
            pltpu.VMEM((tok * heads, width), f32),
            pltpu.VMEM((width, heads * BLOCK), bf16),
            pltpu.VMEM((heads, tok, 256), bf16),
            pltpu.VMEM((heads, BLOCK, 256), bf16),
            pltpu.VMEM((heads * 256, tok), bf16),
            pltpu.VMEM((heads * 256, 2 * width), f32),
            pltpu.VMEM((heads * 256, 2 * width), bf16),
            pltpu.VMEM((heads, tok, width), f32),
            pltpu.VMEM((heads, tok, width), f32),
            pltpu.VMEM((heads, BLOCK, width), f32),
            pltpu.VMEM((heads, BLOCK, width), f32),
            pltpu.VMEM((1, heads * BLOCK), f32),
            pltpu.VMEM((1, heads * BLOCK), f32),
            pltpu.VMEM((width, heads * BLOCK), f32),
            pltpu.VMEM((tok * heads, width), f32),
            pltpu.VMEM((8, width), f32),
            pltpu.VMEM((8, width), f32),
            pltpu.VMEM((2 * nh, 8, width), f32),
            pltpu.VMEM((8, width), f32),
            dma((6,)), dma((n, 2)), dma((2, n, 2)), dma((2,)), dma((2 * nh,)), dma((2 * nh,)), dma((n // 2,)), dma((1,)),
        ],
        compiler_params=pltpu.CompilerParams(
            collective_id=0, has_side_effects=True, vmem_limit_bytes=24 * 1024 * 1024
        ),
    )(*(
        pltpu.with_memory_space_constraint(x, pltpu.HBM) for x in (
            queries.reshape(tok * heads, width), keys.reshape(tok, width), values.reshape(tok, width), feat_q, feat_k, samples,
        )
    ))
    return student.reshape(tok, heads, width), teacher.reshape(1, BLOCK, heads, width), loss.reshape(())


def solution(mesh):
    in_specs = (
        P("seq", "head", None),
        P("seq", "head", None),
        P("seq", "head", None),
        P("head", None, None),
        P("head", None, None),
        P(),
    )
    out_specs = (P("seq", "head", None), P("seq", None, "head", None), P())
    return jax.shard_map(
        functools.partial(on_device, mesh.shape["seq"], mesh.shape["head"]),
        mesh=mesh, in_specs=in_specs, out_specs=out_specs, check_vma=False,
    )
```

```python
import functools

import jax
import jax.numpy as jnp
from jax import lax
from jax.experimental import pallas as pl
from jax.experimental.pallas import tpu as pltpu
from jax.sharding import PartitionSpec as P

BLOCK = 128
MASKED = -1e30
LOG2E = 1.4426950408889634
NT = (((1,), (1,)), ((), ()))


def dot(a, b):
    return jnp.dot(a, b, preferred_element_type=jnp.float32)


def soft_pair(logits, axis):
    logits = logits * LOG2E
    up = jnp.exp2(logits - jnp.max(logits, axis=axis, keepdims=True))
    down = jnp.exp2(jnp.min(logits, axis=axis, keepdims=True) - logits)
    up = up * (1.0 / jnp.sum(up, axis=axis, keepdims=True))
    down = down * (1.0 / jnp.sum(down, axis=axis, keepdims=True))
    return jnp.concatenate([up, down], axis=axis)


def kernel(
    n, nh, q_hbm, k_hbm, v_hbm, fq_hbm, fk_hbm, samples_hbm, student, teacher, loss,
    samples, kv, q_raw, fq, fk, fk_t, rows32, qs_t, phi_q, phi_s, feats, state, state_low, num, den, num_s, den_s, top, tot, acc, out32, column, below, plane, total,
    local_sem, recv_sem, send_sem, up_sem, plane_send, plane_recv, down_send, down_recv,
):
    tok, width = k_hbm.shape
    heads = fq.shape[0]
    s, hd = lax.axis_index("seq"), lax.axis_index("head")
    outer, y = s // 2, s % 2
    last = n // 2 - 1
    partner = s + 1 - 2 * y
    own = (k_hbm, v_hbm)

    local = [
        pltpu.make_async_copy(src, dst, local_sem.at[i])
        for i, (src, dst) in enumerate(
            [(q_hbm, q_raw), (fq_hbm, fq), (fk_hbm, fk), (k_hbm, kv.at[s, 0]), (v_hbm, kv.at[s, 1]),
             (samples_hbm, samples)]
        )
    ]
    for copy in local:
        copy.start()

    barrier = pltpu.get_barrier_semaphore()
    mate = y * nh + hd

    def plane_device(i):
        other = lax.rem(mate + i, 2 * nh)
        return {"seq": 2 * outer + other // nh, "head": lax.rem(other, nh)}

    for i in range(1, 2 * nh):
        pl.semaphore_signal(barrier, inc=1, device_id=plane_device(i), device_id_type=pl.DeviceIdType.MESH)

    @pl.when(outer > 0)
    def _():
        pl.semaphore_signal(barrier, inc=1, device_id={"seq": s - 2}, device_id_type=pl.DeviceIdType.MESH)

    @pl.when(outer < last)
    def _():
        pl.semaphore_signal(barrier, inc=1, device_id={"seq": s + 2}, device_id_type=pl.DeviceIdType.MESH)

    pl.semaphore_wait(barrier, 2 * nh - 1 + jnp.minimum(outer, 1) + jnp.minimum(last - outer, 1))

    def hop(src, slot, j, way, target):
        return pltpu.make_async_remote_copy(
            src_ref=src, dst_ref=kv.at[slot, j], send_sem=send_sem.at[way, slot, j],
            recv_sem=recv_sem.at[slot, j], device_id={"seq": target}, device_id_type=pl.DeviceIdType.MESH,
        )

    @pl.when(outer < last)
    def _():
        for j in range(2):
            hop(own[j], s, j, 0, s + 2).start()

    @pl.when(y == 0)
    def _():
        for j in range(2):
            hop(own[j], s, j, 1, partner).start()


    def chosen(rows):
        block = rows[:BLOCK]
        for b in range(1, tok // BLOCK):
            block = jnp.where(pick == b, rows[b * BLOCK:(b + 1) * BLOCK], block)
        return block

    def key_features(keys):
        logits = lax.dot_general(fk_t[...], keys, NT, preferred_element_type=jnp.float32)
        for h in range(heads):
            feats[h * 256:(h + 1) * 256, :] = soft_pair(logits[h * 128:(h + 1) * 128], 0).astype(jnp.bfloat16)

    def weigh(keys, live):
        out = []
        for c in range(heads // 2):
            cols = slice(c * 2 * BLOCK, (c + 1) * 2 * BLOCK)
            scores = dot(keys, qs_t[:, cols]) * (LOG2E / width ** 0.5)
            if live is not None:
                scores = jnp.where(live, scores, MASKED)
            peak = jnp.max(scores, axis=0, keepdims=True)
            fade = None
            if live is None:
                old = top[:, cols]
                peak = jnp.maximum(old, peak)
                fade = jnp.exp2(old - peak)
            weights = jnp.exp2(scores - peak)
            part = jnp.sum(weights, axis=0, keepdims=True)
            top[:, cols] = peak
            tot[:, cols] = part if live is not None else part + tot[:, cols] * fade
            out.append((cols, weights.astype(jnp.bfloat16), fade))
        return out

    def mix(weighed, values):
        values_t = values.astype(jnp.float32).T.astype(jnp.bfloat16)
        for cols, weights, fade in weighed:
            mixed = dot(values_t, weights)
            acc[:, cols] = mixed if fade is None else mixed + acc[:, cols] * fade

    def arrived(slot, j):
        hop(kv.at[slot, j], slot, j, 0, partner).wait_recv()

    def absorb(slot, wait):
        if wait:
            arrived(slot, 0)
        keys = kv[slot, 0]
        weighed = weigh(keys, None)
        key_features(keys)
        if wait:
            arrived(slot, 1)
        values = kv[slot, 1]
        mix(weighed, values)
        values_wide = jnp.concatenate([values, jnp.ones_like(values)], axis=1)
        state[...] += dot(feats[...], values_wide)

    def relay(d, j):
        @pl.when(outer >= d)
        def _():
            slot = s - 2 * d
            arrived(slot, j)

            @pl.when(outer < last)
            def _():
                hop(kv.at[slot, j], slot, j, 0, s + 2).start()

            if isinstance(d, int) and (d, j) == (1, 1):
                @pl.when(y + last - outer > 0)
                def _():
                    hop(kv.at[slot, j], slot, j, 1, partner).start()
            else:
                hop(kv.at[slot, j], slot, j, 1, partner).start()

    state[...] = jnp.zeros_like(state)
    for copy in local:
        copy.wait()
    pick = samples[s]
    rows32[...] = q_raw[...].astype(jnp.float32)
    for h in range(heads):
        qs_t[:, h * BLOCK:(h + 1) * BLOCK] = chosen(rows32[pl.ds(h, tok, stride=heads), :]).T.astype(jnp.bfloat16)
        fk_t[h * 128:(h + 1) * 128, :] = fk[h].astype(jnp.float32).T.astype(jnp.bfloat16)

    relay(1, 0)
    for h in range(heads):
        mine = rows32[pl.ds(h, tok, stride=heads), :]
        phi = soft_pair(dot(mine.astype(jnp.bfloat16), fq[h]), 1)
        phi_q[h] = phi.astype(jnp.bfloat16)
        phi_s[h] = chosen(phi).astype(jnp.bfloat16)
        if h == heads // 2 - 1:
            relay(1, 1)
    relay(2, 0)

    keys, values = kv[s, 0], kv[s, 1]
    place = lax.broadcasted_iota(jnp.int32, (tok, 2 * BLOCK), 0)
    row = lax.broadcasted_iota(jnp.int32, (tok, 2 * BLOCK), 1) % BLOCK + pick * BLOCK
    mix(weigh(keys, place <= row), values)

    relay(2, 1)

    causal = lax.broadcasted_iota(jnp.int32, (tok, tok), 0) >= lax.broadcasted_iota(jnp.int32, (tok, tok), 1)
    key_features(keys)
    for h in range(heads):
        inner = jnp.where(causal, dot(phi_q[h], feats[h * 256:(h + 1) * 256, :]), 0.0)
        num[h] = dot(inner.astype(jnp.bfloat16), values)
        den[h] = jnp.broadcast_to(jnp.sum(inner, axis=1, keepdims=True), (tok, width))
        num_s[h] = chosen(num[h])
        den_s[h] = chosen(den[h])

    @pl.when(y == 1)
    def _():
        absorb(partner, True)

        @pl.when(outer == last - 1)
        def _():
            hop(kv.at[partner, 1], partner, 1, 0, s + 2).start()

    def lap(d, carry):
        absorb(s - 2 * d, False)

        relay(d + 2, 0)

        @pl.when(d == outer)
        def _():
            absorb(partner - 2, True)

        @pl.when(d > 1)
        def _():
            absorb(partner - 2 * d, True)

        relay(d + 2, 1)
        return carry

    lax.fori_loop(1, outer + 1, lap, 0)

    def finish(h, phi, numer, denom):
        inter = dot(phi[h], state_low[h * 256:(h + 1) * 256, :])
        result = (numer[h] + inter[:, :width]) / (denom[h] + inter[:, width:])
        return result.astype(jnp.bfloat16).astype(jnp.float32)

    state_low[...] = state[...].astype(jnp.bfloat16)
    part = jnp.zeros((8, width), jnp.float32)
    for h in range(heads):
        cols = slice(h * BLOCK, (h + 1) * BLOCK)
        mixed = (acc[:, cols] / tot[:, cols]).T
        teacher[pl.ds(h, BLOCK, stride=heads), :] = mixed
        gap = finish(h, phi_s, num_s, den_s) - mixed
        part = part + jnp.sum((gap * gap).reshape(BLOCK // 8, 8, width), axis=0)

    def send(src, dst, send_sem, recv_sem, device):
        return pltpu.make_async_remote_copy(
            src_ref=src, dst_ref=dst, send_sem=send_sem, recv_sem=recv_sem,
            device_id=device, device_id_type=pl.DeviceIdType.MESH,
        )

    upward = send(column, below, up_sem.at[0], up_sem.at[1], {"seq": s + 2})
    across = [
        send(plane.at[mate], plane.at[mate], plane_send.at[i], plane_recv.at[i], plane_device(i))
        for i in range(1, 2 * nh)
    ]
    downward = [
        send(total, total, down_send.at[i], down_recv.at[0], {"seq": s - 2 * i}) for i in range(1, last + 1)
    ]
    column[...] = part

    @pl.when(outer > 0)
    def _():
        upward.wait_recv()
        column[...] += below[...]

    @pl.when(outer < last)
    def _():
        upward.start()

    @pl.when(outer == last)
    def _():
        plane[mate] = column[...]
        for copy in across:
            copy.start()

    @pl.when(outer == last)
    def _():
        for copy in across:
            copy.wait()
        total[...] = jnp.sum(plane[...], axis=0)
        for copy in downward:
            copy.start()

    for h in range(heads):
        out32[pl.ds(h, tok, stride=heads), :] = finish(h, phi_q, num, den)
    student[...] = out32[...].astype(jnp.bfloat16)

    @pl.when(outer < last)
    def _():
        for j in range(2):
            hop(own[j], s, j, 0, s + 2).wait_send()

    @pl.when(y == 0)
    def _():
        for j in range(2):
            hop(own[j], s, j, 1, partner).wait_send()

    @pl.when(s == 2 * last - 1)
    def _():
        hop(kv.at[partner, 1], partner, 1, 0, s + 2).wait_send()

    def drain(d, carry):
        near = s - 2 * d
        for j in range(2):
            @pl.when(outer < last)
            def _():
                hop(kv.at[near, j], near, j, 0, s + 2).wait_send()

        hop(kv.at[near, 0], near, 0, 1, partner).wait_send()

        @pl.when(y + last - outer + d > 1)
        def _():
            hop(kv.at[near, 1], near, 1, 1, partner).wait_send()
        return carry

    lax.fori_loop(1, outer + 1, drain, 0)

    @pl.when(outer == last)
    def _():
        for copy in downward:
            copy.wait_send()

    @pl.when(outer < last)
    def _():
        upward.wait_send()
        downward[0].wait_recv()

    loss[0, 0] = jnp.sum(total[...]) * (1.0 / (n * nh * BLOCK * heads * width))


def on_device(n, nh, queries, keys, values, feat_q, feat_k, samples):
    tok, heads, width = queries.shape
    bf16, f32 = jnp.bfloat16, jnp.float32
    in_hbm = pl.BlockSpec(memory_space=pltpu.HBM)
    in_vmem = pl.BlockSpec(memory_space=pltpu.VMEM)
    in_smem = pl.BlockSpec(memory_space=pltpu.SMEM)
    dma = pltpu.SemaphoreType.DMA
    student, teacher, loss = pl.pallas_call(
        functools.partial(kernel, n, nh),
        out_shape=(
            jax.ShapeDtypeStruct((tok * heads, width), bf16),
            jax.ShapeDtypeStruct((BLOCK * heads, width), f32),
            jax.ShapeDtypeStruct((1, 1), f32),
        ),
        in_specs=[in_hbm] * 6,
        out_specs=(in_vmem, in_vmem, in_smem),
        scratch_shapes=[
            pltpu.SMEM((n,), jnp.int32),
            pltpu.VMEM((n, 2, tok, width), bf16),
            pltpu.VMEM((tok * heads, width), bf16),
            pltpu.VMEM(feat_q.shape, bf16),
            pltpu.VMEM(feat_k.shape, bf16),
            pltpu.VMEM((heads * 128, width), bf16),
            pltpu.VMEM((tok * heads, width), f32),
            pltpu.VMEM((width, heads * BLOCK), bf16),
            pltpu.VMEM((heads, tok, 256), bf16),
            pltpu.VMEM((heads, BLOCK, 256), bf16),
            pltpu.VMEM((heads * 256, tok), bf16),
            pltpu.VMEM((heads * 256, 2 * width), f32),
            pltpu.VMEM((heads * 256, 2 * width), bf16),
            pltpu.VMEM((heads, tok, width), f32),
            pltpu.VMEM((heads, tok, width), f32),
            pltpu.VMEM((heads, BLOCK, width), f32),
            pltpu.VMEM((heads, BLOCK, width), f32),
            pltpu.VMEM((1, heads * BLOCK), f32),
            pltpu.VMEM((1, heads * BLOCK), f32),
            pltpu.VMEM((width, heads * BLOCK), f32),
            pltpu.VMEM((tok * heads, width), f32),
            pltpu.VMEM((8, width), f32),
            pltpu.VMEM((8, width), f32),
            pltpu.VMEM((2 * nh, 8, width), f32),
            pltpu.VMEM((8, width), f32),
            dma((6,)), dma((n, 2)), dma((2, n, 2)), dma((2,)), dma((2 * nh,)), dma((2 * nh,)), dma((n // 2,)), dma((1,)),
        ],
        compiler_params=pltpu.CompilerParams(
            collective_id=0, has_side_effects=True, vmem_limit_bytes=24 * 1024 * 1024
        ),
    )(*(
        pltpu.with_memory_space_constraint(x, pltpu.HBM) for x in (
            queries.reshape(tok * heads, width), keys.reshape(tok, width), values.reshape(tok, width), feat_q, feat_k, samples,
        )
    ))
    return student.reshape(tok, heads, width), teacher.reshape(1, BLOCK, heads, width), loss.reshape(())


def solution(mesh):
    in_specs = (
        P("seq", "head", None),
        P("seq", "head", None),
        P("seq", "head", None),
        P("head", None, None),
        P("head", None, None),
        P(),
    )
    out_specs = (P("seq", "head", None), P("seq", None, "head", None), P())
    return jax.shard_map(
        functools.partial(on_device, mesh.shape["seq"], mesh.shape["head"]),
        mesh=mesh, in_specs=in_specs, out_specs=out_specs, check_vma=False,
    )
```

```python
import functools

import jax
import jax.numpy as jnp
from jax import lax
from jax.experimental import pallas as pl
from jax.experimental.pallas import tpu as pltpu
from jax.sharding import PartitionSpec as P

BLOCK = 128
MASKED = -1e30
LOG2E = 1.4426950408889634
NT = (((1,), (1,)), ((), ()))


def dot(a, b):
    return jnp.dot(a, b, preferred_element_type=jnp.float32)


def soft_pair(logits, axis):
    logits = logits * LOG2E
    up = jnp.exp2(logits - jnp.max(logits, axis=axis, keepdims=True))
    down = jnp.exp2(jnp.min(logits, axis=axis, keepdims=True) - logits)
    up = up * (1.0 / jnp.sum(up, axis=axis, keepdims=True))
    down = down * (1.0 / jnp.sum(down, axis=axis, keepdims=True))
    return jnp.concatenate([up, down], axis=axis)


def kernel(
    n, nh, q_hbm, k_hbm, v_hbm, fq_hbm, fk_hbm, samples_hbm, student, teacher, loss,
    samples, kv, q_raw, fq, fk, fk_t, rows32, qs_t, phi_q, phi_s, feats, state, state_low, num, den, num_s, den_s, top, tot, acc, out32, column, below, plane, total,
    local_sem, recv_sem, send_sem, up_sem, plane_send, plane_recv, down_send, down_recv,
):
    tok, width = k_hbm.shape
    heads = fq.shape[0]
    s, hd = lax.axis_index("seq"), lax.axis_index("head")
    outer, y = s // 2, s % 2
    last = n // 2 - 1
    partner = s + 1 - 2 * y
    half = tok // 2
    own = [x.at[i * half:(i + 1) * half, :] for x in (k_hbm, v_hbm) for i in range(2)]

    local = [
        pltpu.make_async_copy(src, dst, local_sem.at[i])
        for i, (src, dst) in enumerate(
            [(q_hbm, q_raw), (fq_hbm, fq), (fk_hbm, fk), (samples_hbm, samples)]
            + [(own[p], kv.at[s, p]) for p in range(4)]
        )
    ]
    for copy in local:
        copy.start()

    barrier = pltpu.get_barrier_semaphore()
    mate = y * nh + hd

    def plane_device(i):
        other = lax.rem(mate + i, 2 * nh)
        return {"seq": 2 * outer + other // nh, "head": lax.rem(other, nh)}

    for i in range(1, 2 * nh):
        pl.semaphore_signal(barrier, inc=1, device_id=plane_device(i), device_id_type=pl.DeviceIdType.MESH)

    @pl.when(outer > 0)
    def _():
        pl.semaphore_signal(barrier, inc=1, device_id={"seq": s - 2}, device_id_type=pl.DeviceIdType.MESH)

    @pl.when(outer < last)
    def _():
        pl.semaphore_signal(barrier, inc=1, device_id={"seq": s + 2}, device_id_type=pl.DeviceIdType.MESH)

    pl.semaphore_wait(barrier, 2 * nh - 1 + jnp.minimum(outer, 1) + jnp.minimum(last - outer, 1))

    def hop(src, slot, j, way, target):
        return pltpu.make_async_remote_copy(
            src_ref=src, dst_ref=kv.at[slot, j], send_sem=send_sem.at[way, slot, j],
            recv_sem=recv_sem.at[slot, j], device_id={"seq": target}, device_id_type=pl.DeviceIdType.MESH,
        )

    @pl.when(outer < last)
    def _():
        for j in range(4):
            hop(own[j], s, j, 0, s + 2).start()

    @pl.when(y == 0)
    def _():
        for j in range(4):
            hop(own[j], s, j, 1, partner).start()


    def chosen(rows):
        block = rows[:BLOCK]
        for b in range(1, tok // BLOCK):
            block = jnp.where(pick == b, rows[b * BLOCK:(b + 1) * BLOCK], block)
        return block

    def key_features(keys):
        logits = lax.dot_general(fk_t[...], keys, NT, preferred_element_type=jnp.float32)
        for h in range(heads):
            feats[h * 256:(h + 1) * 256, :] = soft_pair(logits[h * 128:(h + 1) * 128], 0).astype(jnp.bfloat16)

    def weigh(keys, live):
        out = []
        for c in range(heads // 2):
            cols = slice(c * 2 * BLOCK, (c + 1) * 2 * BLOCK)
            scores = dot(keys, qs_t[:, cols]) * (LOG2E / width ** 0.5)
            if live is not None:
                scores = jnp.where(live, scores, MASKED)
            peak = jnp.max(scores, axis=0, keepdims=True)
            fade = None
            if live is None:
                old = top[:, cols]
                peak = jnp.maximum(old, peak)
                fade = jnp.exp2(old - peak)
            weights = jnp.exp2(scores - peak)
            part = jnp.sum(weights, axis=0, keepdims=True)
            top[:, cols] = peak
            tot[:, cols] = part if live is not None else part + tot[:, cols] * fade
            out.append((cols, weights.astype(jnp.bfloat16), fade))
        return out

    def mix(weighed, values):
        values_t = values.astype(jnp.float32).T.astype(jnp.bfloat16)
        for cols, weights, fade in weighed:
            mixed = dot(values_t, weights)
            acc[:, cols] = mixed if fade is None else mixed + acc[:, cols] * fade

    def arrived(slot, j):
        for p in (2 * j, 2 * j + 1):
            hop(kv.at[slot, p], slot, p, 0, partner).wait_recv()

    def rows(slot, j):
        return kv[slot, 2 * j:2 * j + 2].reshape(tok, width)

    def absorb(slot, wait):
        if wait:
            arrived(slot, 0)
        keys = rows(slot, 0)
        weighed = weigh(keys, None)
        key_features(keys)
        if wait:
            arrived(slot, 1)
        values = rows(slot, 1)
        mix(weighed, values)
        values_wide = jnp.concatenate([values, jnp.ones_like(values)], axis=1)
        state[...] += dot(feats[...], values_wide)

    def relay(d, j):
        def hand_on(p):
            slot = s - 2 * d
            hop(kv.at[slot, p], slot, p, 0, partner).wait_recv()

            @pl.when(outer < last)
            def _():
                hop(kv.at[slot, p], slot, p, 0, s + 2).start()

            if isinstance(d, int) and (d, j) == (1, 1):
                @pl.when(y + last - outer > 0)
                def _():
                    hop(kv.at[slot, p], slot, p, 1, partner).start()
            else:
                hop(kv.at[slot, p], slot, p, 1, partner).start()

        @pl.when(outer >= d)
        def _():
            hand_on(2 * j)
            hand_on(2 * j + 1)

    state[...] = jnp.zeros_like(state)
    for copy in local:
        copy.wait()
    pick = samples[s]
    rows32[...] = q_raw[...].astype(jnp.float32)
    for h in range(heads):
        qs_t[:, h * BLOCK:(h + 1) * BLOCK] = chosen(rows32[pl.ds(h, tok, stride=heads), :]).T.astype(jnp.bfloat16)
        fk_t[h * 128:(h + 1) * 128, :] = fk[h].astype(jnp.float32).T.astype(jnp.bfloat16)

    relay(1, 0)
    for h in range(heads):
        mine = rows32[pl.ds(h, tok, stride=heads), :]
        phi = soft_pair(dot(mine.astype(jnp.bfloat16), fq[h]), 1)
        phi_q[h] = phi.astype(jnp.bfloat16)
        phi_s[h] = chosen(phi).astype(jnp.bfloat16)
        if h == heads // 2 - 1:
            relay(1, 1)
    relay(2, 0)

    keys, values = rows(s, 0), rows(s, 1)
    place = lax.broadcasted_iota(jnp.int32, (tok, 2 * BLOCK), 0)
    row = lax.broadcasted_iota(jnp.int32, (tok, 2 * BLOCK), 1) % BLOCK + pick * BLOCK
    mix(weigh(keys, place <= row), values)

    relay(2, 1)

    causal = lax.broadcasted_iota(jnp.int32, (tok, tok), 0) >= lax.broadcasted_iota(jnp.int32, (tok, tok), 1)
    key_features(keys)
    for h in range(heads):
        inner = jnp.where(causal, dot(phi_q[h], feats[h * 256:(h + 1) * 256, :]), 0.0)
        num[h] = dot(inner.astype(jnp.bfloat16), values)
        den[h] = jnp.broadcast_to(jnp.sum(inner, axis=1, keepdims=True), (tok, width))
        num_s[h] = chosen(num[h])
        den_s[h] = chosen(den[h])

    @pl.when(y == 1)
    def _():
        absorb(partner, True)

        @pl.when(outer == last - 1)
        def _():
            for p in (2, 3):
                hop(kv.at[partner, p], partner, p, 0, s + 2).start()

    def lap(d, carry):
        absorb(s - 2 * d, False)

        relay(d + 2, 0)

        @pl.when(d == outer)
        def _():
            absorb(partner - 2, True)

        @pl.when(d > 1)
        def _():
            absorb(partner - 2 * d, True)

        relay(d + 2, 1)
        return carry

    lax.fori_loop(1, outer + 1, lap, 0)

    def finish(h, phi, numer, denom):
        inter = dot(phi[h], state_low[h * 256:(h + 1) * 256, :])
        result = (numer[h] + inter[:, :width]) / (denom[h] + inter[:, width:])
        return result.astype(jnp.bfloat16).astype(jnp.float32)

    state_low[...] = state[...].astype(jnp.bfloat16)
    part = jnp.zeros((8, width), jnp.float32)
    for h in range(heads):
        cols = slice(h * BLOCK, (h + 1) * BLOCK)
        mixed = (acc[:, cols] / tot[:, cols]).T
        teacher[pl.ds(h, BLOCK, stride=heads), :] = mixed
        gap = finish(h, phi_s, num_s, den_s) - mixed
        part = part + jnp.sum((gap * gap).reshape(BLOCK // 8, 8, width), axis=0)

    def send(src, dst, send_sem, recv_sem, device):
        return pltpu.make_async_remote_copy(
            src_ref=src, dst_ref=dst, send_sem=send_sem, recv_sem=recv_sem,
            device_id=device, device_id_type=pl.DeviceIdType.MESH,
        )

    upward = send(column, below, up_sem.at[0], up_sem.at[1], {"seq": s + 2})
    across = [
        send(plane.at[mate], plane.at[mate], plane_send.at[i], plane_recv.at[i], plane_device(i))
        for i in range(1, 2 * nh)
    ]
    downward = [
        send(total, total, down_send.at[i], down_recv.at[0], {"seq": s - 2 * i}) for i in range(1, last + 1)
    ]
    column[...] = part

    @pl.when(outer > 0)
    def _():
        upward.wait_recv()
        column[...] += below[...]

    @pl.when(outer < last)
    def _():
        upward.start()

    @pl.when(outer == last)
    def _():
        plane[mate] = column[...]
        for copy in across:
            copy.start()

    @pl.when(outer == last)
    def _():
        for copy in across:
            copy.wait()
        total[...] = jnp.sum(plane[...], axis=0)
        for copy in downward:
            copy.start()

    for h in range(heads):
        out32[pl.ds(h, tok, stride=heads), :] = finish(h, phi_q, num, den)
    student[...] = out32[...].astype(jnp.bfloat16)

    @pl.when(outer < last)
    def _():
        for j in range(4):
            hop(own[j], s, j, 0, s + 2).wait_send()

    @pl.when(y == 0)
    def _():
        for j in range(4):
            hop(own[j], s, j, 1, partner).wait_send()

    @pl.when(s == 2 * last - 1)
    def _():
        for p in (2, 3):
            hop(kv.at[partner, p], partner, p, 0, s + 2).wait_send()

    def drain(d, carry):
        near = s - 2 * d
        @pl.when(outer < last)
        def _():
            for p in range(4):
                hop(kv.at[near, p], near, p, 0, s + 2).wait_send()

        for p in range(2):
            hop(kv.at[near, p], near, p, 1, partner).wait_send()

        @pl.when(y + last - outer + d > 1)
        def _():
            for p in (2, 3):
                hop(kv.at[near, p], near, p, 1, partner).wait_send()
        return carry

    lax.fori_loop(1, outer + 1, drain, 0)

    @pl.when(outer == last)
    def _():
        for copy in downward:
            copy.wait_send()

    @pl.when(outer < last)
    def _():
        upward.wait_send()
        downward[0].wait_recv()

    loss[0, 0] = jnp.sum(total[...]) * (1.0 / (n * nh * BLOCK * heads * width))


def on_device(n, nh, queries, keys, values, feat_q, feat_k, samples):
    tok, heads, width = queries.shape
    bf16, f32 = jnp.bfloat16, jnp.float32
    in_hbm = pl.BlockSpec(memory_space=pltpu.HBM)
    in_vmem = pl.BlockSpec(memory_space=pltpu.VMEM)
    in_smem = pl.BlockSpec(memory_space=pltpu.SMEM)
    dma = pltpu.SemaphoreType.DMA
    student, teacher, loss = pl.pallas_call(
        functools.partial(kernel, n, nh),
        out_shape=(
            jax.ShapeDtypeStruct((tok * heads, width), bf16),
            jax.ShapeDtypeStruct((BLOCK * heads, width), f32),
            jax.ShapeDtypeStruct((1, 1), f32),
        ),
        in_specs=[in_hbm] * 6,
        out_specs=(in_vmem, in_vmem, in_smem),
        scratch_shapes=[
            pltpu.SMEM((n,), jnp.int32),
            pltpu.VMEM((n, 4, tok // 2, width), bf16),
            pltpu.VMEM((tok * heads, width), bf16),
            pltpu.VMEM(feat_q.shape, bf16),
            pltpu.VMEM(feat_k.shape, bf16),
            pltpu.VMEM((heads * 128, width), bf16),
            pltpu.VMEM((tok * heads, width), f32),
            pltpu.VMEM((width, heads * BLOCK), bf16),
            pltpu.VMEM((heads, tok, 256), bf16),
            pltpu.VMEM((heads, BLOCK, 256), bf16),
            pltpu.VMEM((heads * 256, tok), bf16),
            pltpu.VMEM((heads * 256, 2 * width), f32),
            pltpu.VMEM((heads * 256, 2 * width), bf16),
            pltpu.VMEM((heads, tok, width), f32),
            pltpu.VMEM((heads, tok, width), f32),
            pltpu.VMEM((heads, BLOCK, width), f32),
            pltpu.VMEM((heads, BLOCK, width), f32),
            pltpu.VMEM((1, heads * BLOCK), f32),
            pltpu.VMEM((1, heads * BLOCK), f32),
            pltpu.VMEM((width, heads * BLOCK), f32),
            pltpu.VMEM((tok * heads, width), f32),
            pltpu.VMEM((8, width), f32),
            pltpu.VMEM((8, width), f32),
            pltpu.VMEM((2 * nh, 8, width), f32),
            pltpu.VMEM((8, width), f32),
            dma((8,)), dma((n, 4)), dma((2, n, 4)), dma((2,)), dma((2 * nh,)), dma((2 * nh,)), dma((n // 2,)), dma((1,)),
        ],
        compiler_params=pltpu.CompilerParams(
            collective_id=0, has_side_effects=True, vmem_limit_bytes=24 * 1024 * 1024
        ),
    )(*(
        pltpu.with_memory_space_constraint(x, pltpu.HBM) for x in (
            queries.reshape(tok * heads, width), keys.reshape(tok, width), values.reshape(tok, width), feat_q, feat_k, samples,
        )
    ))
    return student.reshape(tok, heads, width), teacher.reshape(1, BLOCK, heads, width), loss.reshape(())


def solution(mesh):
    in_specs = (
        P("seq", "head", None),
        P("seq", "head", None),
        P("seq", "head", None),
        P("head", None, None),
        P("head", None, None),
        P(),
    )
    out_specs = (P("seq", "head", None), P("seq", None, "head", None), P())
    return jax.shard_map(
        functools.partial(on_device, mesh.shape["seq"], mesh.shape["head"]),
        mesh=mesh, in_specs=in_specs, out_specs=out_specs, check_vma=False,
    )
```
